32 devices in a mesh: row: 8 (over y, x, core), layer: 4 (over z).
Axes of the slice: x: 2, y: 2, z: 4, core: 2. Of those that a mesh axis runs over, the one named last changes fastest.
Arguments:
- rhs_local: bfloat16 [4, 2, 1024, 256], P('layer', None, 'row'), may hold values from -6 to 6
- dinv_local: bfloat16 [4, 2, 1024, 1024], P('layer', None, 'row')
- lower_anc: bfloat16 [4, 2, 1024, 1024], P('layer', None, 'row'), may hold values from -0.0625 to 0.0625
- lower_high: bfloat16 [4, 2, 8192, 1024], P('layer', None, 'row'), may hold values from -0.09375 to 0.09375
- row_blocks: int32 [4, 2, 64], P('layer', None, 'row'), may hold values from 0 to 15
- rhs_anc: float32 [1024, 256], P('row'), may hold values from -6 to 6
- rhs_high: float32 [16384, 256], P(('row', 'layer')), may hold values from -6 to 6
- dinv_anc: bfloat16 [1024, 1024], P('row')
- lower_anc_high: bfloat16 [16384, 1024], P(('row', 'layer')), may hold values from -0.1875 to 0.1875
Outputs:
- sol_local: bfloat16 [4, 2, 1024, 256], P('layer', None, 'row')
- sol_anc: bfloat16 [1024, 256], P('row')
- high_out: float32 [16384, 256], P(('row', 'layer'))
The draws below stay inside these ranges and needn't reach their ends.
Inputs may be any that keep to these rules, and one draw needn't show every extreme that they name: Row index block q of lower_high, held by row index g = q // 8, lands in block row_blocks of that index's 16 blocks of higher ancestor rows.
All inputs are finite; a program needn't handle non-finite values.
Results may differ from the reference program's by a relative error of at most 0.008.
Values may be sent and summed in bfloat16 or wider, within the bound.
No kernel may reach another device: no remote copies, remote signals or barrier semaphores. Data moves between devices by JAX's collectives and lax.ppermute only.
A program may use at most 64 MiB of HBM per device.

```python
import math
import jax
import jax.numpy as jnp
from jax import lax

NS = 1024
RHS = 256
NA = 1024
SN = 2
BLOCK = 128
HBLK = 16
LBLK = 8
N_ROW = 8
N_LAYER = 4


def inverse_blocks(key, shape, order):
    noise = jax.random.normal(key, shape, jnp.float32)
    return jnp.eye(order, dtype=jnp.float32) + 0.6 * noise / math.sqrt(order)


def draw_dinv_local(key, part):
    folded = jax.random.fold_in(key, 11)
    return inverse_blocks(folded, (N_LAYER, SN, NS, NS), NS).astype(jnp.bfloat16)


def draw_dinv_anc(key, part):
    folded = jax.random.fold_in(key, 23)
    return inverse_blocks(folded, (NA, NA), NA).astype(jnp.bfloat16)


def plant(entries, rng, least, top_value):
    spot = [jax.random.randint(jax.random.fold_in(rng, axis), (), 0, length) for axis, length in enumerate(entries.shape)]
    longest = entries.shape.index(max(entries.shape))
    next_to = spot[:longest] + [(spot[longest] + 1) % entries.shape[longest]] + spot[longest + 1:]
    return entries.at[tuple(spot)].set(least).at[tuple(next_to)].set(top_value)


def block_scale(stream_key, dims, cuts, least, high):
    gain = 1.0
    for axis_at, parts in cuts:
        draws = jax.random.uniform(jax.random.fold_in(jax.random.fold_in(stream_key, 6), axis_at), (parts,), jnp.float32, least / len(cuts), high / len(cuts))
        gain = gain * jnp.repeat(jnp.exp(draws), dims[axis_at] // parts).reshape((-1,) + (1,) * (len(dims) - 1 - axis_at))
    return gain


def gaussian(own_key, shape, deviation, bound, split=(), held_as=jnp.bfloat16):
    result = jax.random.normal(own_key, shape, jnp.float32) * deviation
    if len(split) > 0:
        result = block_scale(own_key, shape, split, -0.22, 0.18) * result
    return jnp.clip(result, min=-bound, max=bound).astype(held_as)


def setup_inputs(seed: int = 0) -> dict:
    streams_of = jax.random.split(jax.random.key(seed), 10)
    rhs_local = gaussian(streams_of[0], (N_LAYER, SN, NS, RHS), 1.0, 6.0, ((0, 4), (2, 8)))
    dinv_local = draw_dinv_local(jax.random.fold_in(streams_of[9], 71), 0)
    lower_anc = gaussian(streams_of[2], (N_LAYER, SN, NA, NS), (NS * SN * N_LAYER) ** -0.5, 0.0625, ((0, 4), (2, 8)))
    lower_high = gaussian(streams_of[3], (N_LAYER, SN, N_ROW * LBLK * BLOCK, NS), (NS * N_LAYER) ** -0.5, 0.09375, ((0, 4), (2, 8)))
    row_blocks = plant(jax.random.randint(streams_of[4], (N_LAYER, SN, N_ROW * LBLK), 0, HBLK), jax.random.fold_in(streams_of[4], 1), 0, HBLK - 1).astype(jnp.int32)
    rhs_anc = gaussian(streams_of[5], (NA, RHS), 1.0, 6.0, ((0, 8),), jnp.float32)
    rhs_high = gaussian(streams_of[6], (N_ROW * HBLK * BLOCK, RHS), 1.0, 6.0, ((0, 32),), jnp.float32)
    dinv_anc = draw_dinv_anc(jax.random.fold_in(streams_of[9], 71), 0)
    lower_anc_high = gaussian(streams_of[8], (N_ROW * HBLK * BLOCK, NA), NA ** -0.5, 0.1875, ((0, 32),))
    return dict(rhs_local=rhs_local, dinv_local=dinv_local, lower_anc=lower_anc, lower_high=lower_high, row_blocks=row_blocks, rhs_anc=rhs_anc, rhs_high=rhs_high, dinv_anc=dinv_anc, lower_anc_high=lower_anc_high)


def reference(rhs_local, dinv_local, lower_anc, lower_high, row_blocks, rhs_anc, rhs_high, dinv_anc, lower_anc_high):
    high_total = N_ROW * HBLK * BLOCK
    positions = jnp.arange(N_ROW * LBLK * BLOCK, dtype=jnp.int32)
    owner = (positions // (LBLK * BLOCK)).astype(jnp.int32)
    block_index = (positions // BLOCK).astype(jnp.int32)
    within = (positions % BLOCK).astype(jnp.int32)

    def one_layer(carry, items):
        anc_total, high_sum = carry
        rhs_one, dinv_one, anc_one, high_one, blocks_one = items
        solved = jnp.einsum("sik,skc->sic", dinv_one.astype(jnp.float32), rhs_one.astype(jnp.float32)).astype(jnp.bfloat16)
        solved_wide = solved.astype(jnp.float32)
        anc_total = anc_total + jnp.einsum("sik,skc->ic", anc_one.astype(jnp.float32), solved_wide)
        contrib = jnp.einsum("sik,skc->sic", high_one.astype(jnp.float32), solved_wide)
        targets = (owner[None, :] * (HBLK * BLOCK) + blocks_one[:, block_index] * BLOCK + within[None, :]).astype(jnp.int32)
        high_sum = high_sum.at[targets.reshape(-1)].add(contrib.reshape(-1, RHS))
        return (anc_total, high_sum), solved

    start = (jnp.zeros((NA, RHS), jnp.float32), jnp.zeros((high_total, RHS), jnp.float32))
    (anc_update, high_update), sol_local = lax.scan(one_layer, start, (rhs_local, dinv_local, lower_anc, lower_high, row_blocks))
    anc_rhs = (rhs_anc - anc_update).astype(jnp.bfloat16)
    sol_anc = jnp.dot(dinv_anc, anc_rhs, preferred_element_type=jnp.float32).astype(jnp.bfloat16)
    high_out = rhs_high - high_update - jnp.dot(lower_anc_high, sol_anc, preferred_element_type=jnp.float32)
    return sol_local, sol_anc, high_out
```

```python
import functools

import jax
import jax.numpy as jnp
from jax import lax
from jax.experimental import pallas as pl
from jax.experimental.pallas import tpu as pltpu
from jax.sharding import PartitionSpec as P

F32 = jnp.float32
BF16 = jnp.bfloat16
VMEM = pl.BlockSpec(memory_space=pltpu.VMEM)
SMEM = pl.BlockSpec(memory_space=pltpu.SMEM)


def swap(value, axis, size, mask):
    return lax.ppermute(value, axis, [(i, i ^ mask) for i in range(size)])


def gather_row(value, size):
    blocks = {0: value}
    for mask in range(2, size, 2):
        blocks[mask] = swap(value, "row", size, mask)
    blocks[1] = swap(value, "row", size, 1)
    for mask in range(2, size, 2):
        blocks[mask + 1] = swap(blocks[mask], "row", size, 1)
    return [blocks[mask] for mask in range(size)]


def call(body, outs, scratch, specs, operands, flops):
    moved = sum(o.size * o.dtype.itemsize for o in operands)
    return pl.pallas_call(
        body,
        out_shape=outs,
        in_specs=specs,
        out_specs=jax.tree.map(lambda _: VMEM, outs),
        scratch_shapes=scratch,
        cost_estimate=pl.CostEstimate(flops=flops, bytes_accessed=moved, transcendentals=0),
        compiler_params=pltpu.CompilerParams(vmem_limit_bytes=32 * 1024 * 1024),
    )(*operands)


def place(me_ref, blocks, full_ref, rows):
    for mask, block in enumerate(blocks):
        at = pl.multiple_of((me_ref[0] ^ mask) * rows, rows)
        if len(full_ref.shape) == 3:
            full_ref[:, pl.ds(at, rows), :] = block[...]
        else:
            full_ref[pl.ds(at, rows), :] = block[...]


def dot(left, right):
    return jnp.dot(left, right, preferred_element_type=F32)


def solve_local(size, me_ref, matrix_ref, *refs):
    blocks, (out_ref, full_ref) = refs[:size], refs[size:]
    place(me_ref, blocks, full_ref, blocks[0].shape[1])
    for s in range(matrix_ref.shape[0]):
        out_ref[s] = dot(matrix_ref[s], full_ref[s]).astype(BF16)


def reach_anc(size, me_ref, matrix_ref, *refs):
    blocks, (out_ref, full_ref) = refs[:size], refs[size:]
    place(me_ref, blocks, full_ref, blocks[0].shape[1])
    total = dot(matrix_ref[0], full_ref[0])
    for s in range(1, matrix_ref.shape[0]):
        total = total + dot(matrix_ref[s], full_ref[s])
    out_ref[...] = total.astype(BF16)


def reach_high(layers, block, me_ref, target_ref, matrix_ref, full_ref, *refs):
    outs, total_ref = refs[:layers], refs[layers]
    total_ref[...] = jnp.zeros_like(total_ref)
    supers, rows, _ = matrix_ref.shape
    for s in range(supers):
        for q in range(rows // block):
            at = pl.multiple_of(target_ref[s, q] * block, block)
            total_ref[pl.ds(at, block), :] += dot(matrix_ref[s, q * block : (q + 1) * block, :], full_ref[s])
    part = total_ref.shape[0] // layers
    for mask in range(layers):
        at = pl.multiple_of((me_ref[0] ^ mask) * part, part)
        outs[mask][...] = total_ref[pl.ds(at, part), :].astype(BF16)


def tree(values):
    while len(values) > 1:
        values = [values[i] + values[i + 1] for i in range(0, len(values), 2)]
    return values[0]


def reduce_anc(layers, rhs_ref, *refs):
    out_ref = refs[layers]
    out_ref[...] = (rhs_ref[...] - tree([part[...].astype(F32) for part in refs[:layers]])).astype(BF16)


def solve_anc(size, me_ref, matrix_ref, *refs):
    blocks, (out_ref, full_ref) = refs[:size], refs[size:]
    place(me_ref, blocks, full_ref, blocks[0].shape[0])
    out_ref[...] = dot(matrix_ref[...], full_ref[...]).astype(BF16)


def finish(size, layers, me_ref, matrix_ref, rhs_ref, *refs):
    blocks, parts, (out_ref, full_ref) = refs[:size], refs[size : size + layers], refs[size + layers :]
    place(me_ref, blocks, full_ref, blocks[0].shape[0])
    high = tree([part[...].astype(F32) for part in parts])
    out_ref[...] = rhs_ref[...] - high - dot(matrix_ref[...], full_ref[...])


def on_device(
    rows_n,
    layers_n,
    rhs_local,
    dinv_local,
    lower_anc,
    lower_high,
    row_blocks,
    rhs_anc,
    rhs_high,
    dinv_anc,
    lower_anc_high,
):
    rhs_mine, dinv_mine, anc_mine = rhs_local[0], dinv_local[0], lower_anc[0]
    high_mine, blocks_mine = lower_high[0], row_blocks[0]
    supers, order, width = rhs_mine.shape[0], dinv_mine.shape[2], rhs_mine.shape[2]
    block = high_mine.shape[1] // blocks_mine.shape[1]
    held = rhs_high.shape[0]
    me_row = lax.axis_index("row").astype(jnp.int32).reshape(1)
    me_layer = lax.axis_index("layer").astype(jnp.int32).reshape(1)
    shape = jax.ShapeDtypeStruct
    full = (supers, order, width)

    rhs_blocks = gather_row(rhs_mine, rows_n)
    sol_mine = call(
        functools.partial(solve_local, rows_n),
        shape(rhs_mine.shape, BF16),
        [pltpu.VMEM(full, BF16)],
        [SMEM] + [VMEM] * (1 + rows_n),
        (me_row, dinv_mine, *rhs_blocks),
        2 * dinv_mine.size * width,
    )
    sol_blocks = gather_row(sol_mine, rows_n)
    anc_part, sol_full = call(
        functools.partial(reach_anc, rows_n),
        (shape((anc_mine.shape[1], width), BF16), shape(full, BF16)),
        [],
        [SMEM] + [VMEM] * (1 + rows_n),
        (me_row, anc_mine, *sol_blocks),
        2 * anc_mine.size * width,
    )
    anc_parts = [anc_part] + [swap(anc_part, "layer", layers_n, mask) for mask in range(1, layers_n)]
    high_parts = call(
        functools.partial(reach_high, layers_n, block),
        [shape((held, width), BF16)] * layers_n,
        [pltpu.VMEM((held * layers_n, width), F32)],
        [SMEM, SMEM] + [VMEM] * 2,
        (me_layer, blocks_mine, high_mine, sol_full),
        2 * high_mine.size * width,
    )
    high_parts = [high_parts[0]] + [
        swap(high_parts[mask], "layer", layers_n, mask) for mask in range(1, layers_n)
    ]
    anc_rhs = call(
        functools.partial(reduce_anc, layers_n),
        shape(rhs_anc.shape, BF16),
        [],
        [VMEM] * (1 + layers_n),
        (rhs_anc, *anc_parts),
        rhs_anc.size * layers_n,
    )
    anc_solved = call(
        functools.partial(solve_anc, rows_n),
        shape(rhs_anc.shape, BF16),
        [pltpu.VMEM((dinv_anc.shape[1], width), BF16)],
        [SMEM] + [VMEM] * (1 + rows_n),
        (me_row, dinv_anc, *gather_row(anc_rhs, rows_n)),
        2 * dinv_anc.size * width,
    )
    high_new = call(
        functools.partial(finish, rows_n, layers_n),
        shape(rhs_high.shape, F32),
        [pltpu.VMEM((lower_anc_high.shape[1], width), BF16)],
        [SMEM] + [VMEM] * (2 + rows_n + layers_n),
        (me_row, lower_anc_high, rhs_high, *gather_row(anc_solved, rows_n), *high_parts),
        2 * lower_anc_high.size * width,
    )
    return (sol_mine[None], anc_solved, high_new)


def solution(mesh):
    return jax.shard_map(
        functools.partial(on_device, mesh.shape["row"], mesh.shape["layer"]),
        mesh=mesh,
        in_specs=(
            P("layer", None, "row", None),
            P("layer", None, "row", None),
            P("layer", None, "row", None),
            P("layer", None, "row", None),
            P("layer", None, "row"),
            P("row", None),
            P(("row", "layer"), None),
            P("row", None),
            P(("row", "layer"), None),
        ),
        out_specs=(P("layer", None, "row", None), P("row", None), P(("row", "layer"), None)),
        check_vma=False,
    )
```

```python
import functools

import jax
import jax.numpy as jnp
from jax import lax
from jax.experimental import pallas as pl
from jax.experimental.pallas import tpu as pltpu
from jax.sharding import PartitionSpec as P

F32 = jnp.float32
BF16 = jnp.bfloat16
VMEM = pl.BlockSpec(memory_space=pltpu.VMEM)
SMEM = pl.BlockSpec(memory_space=pltpu.SMEM)
ANY = pl.BlockSpec(memory_space=pl.ANY)
HBM = pl.BlockSpec(memory_space=pltpu.HBM)


def swap(value, axis, size, mask):
    return lax.ppermute(value, axis, [(i, i ^ mask) for i in range(size)])


def gather_row(value, size, after=None):
    blocks = {0: value}
    for mask in range(2, size, 2):
        blocks[mask] = swap(value, "row", size, mask)
    blocks[1] = swap(value, "row", size, 1)
    for mask in range(2, size, 2):
        if after is not None:
            blocks[mask], _ = lax.optimization_barrier((blocks[mask], after))
        blocks[mask + 1] = swap(blocks[mask], "row", size, 1)
    return [blocks[mask] for mask in range(size)]


def call(body, outs, operands, scalars=(), scratch=(), flops=0, after=(), spec=VMEM, limit=16):
    count, waits = len(scalars) + len(operands), len(after)

    def kernel(*refs):
        body(*refs[:count], *refs[count + waits :])

    moved = sum(o.size * o.dtype.itemsize for o in operands)
    return pl.pallas_call(
        kernel,
        out_shape=outs,
        in_specs=[SMEM] * len(scalars) + [spec] * len(operands) + [ANY] * waits,
        out_specs=jax.tree.map(lambda _: VMEM, outs),
        scratch_shapes=list(scratch),
        cost_estimate=pl.CostEstimate(flops=flops, bytes_accessed=moved, transcendentals=0),
        compiler_params=pltpu.CompilerParams(vmem_limit_bytes=limit * 1024 * 1024),
    )(*scalars, *operands, *after)


def stage(count, *refs):
    sems = refs[2 * count]
    copies = [pltpu.make_async_copy(refs[i], refs[count + i], sems.at[i]) for i in range(count)]
    for copy in copies:
        copy.start()
    for copy in copies:
        copy.wait()


def emit(count, *refs):
    for i in range(count):
        refs[count + i][...] = refs[i][...]


def place(me_ref, blocks, full_ref, rows):
    for mask, block in enumerate(blocks):
        at = pl.multiple_of((me_ref[0] ^ mask) * rows, rows)
        if len(full_ref.shape) == 3:
            full_ref[:, pl.ds(at, rows), :] = block[...]
        else:
            full_ref[pl.ds(at, rows), :] = block[...]


def dot(left, right):
    return jnp.dot(left, right, preferred_element_type=F32)


def solve_local(size, me_ref, matrix_ref, *refs):
    blocks, (out_ref, full_ref) = refs[:size], refs[size:]
    place(me_ref, blocks, full_ref, blocks[0].shape[1])
    for s in range(matrix_ref.shape[0]):
        out_ref[s] = dot(matrix_ref[s], full_ref[s]).astype(BF16)


def reach_anc(size, me_ref, matrix_ref, *refs):
    blocks, (out_ref, full_ref) = refs[:size], refs[size:]
    place(me_ref, blocks, full_ref, blocks[0].shape[1])
    total = dot(matrix_ref[0], full_ref[0])
    for s in range(1, matrix_ref.shape[0]):
        total = total + dot(matrix_ref[s], full_ref[s])
    out_ref[...] = total.astype(BF16)


def reach_high(layers, block, me_ref, target_ref, matrix_ref, full_ref, *refs):
    outs, total_ref = refs[:layers], refs[layers]
    total_ref[...] = jnp.zeros_like(total_ref)
    supers, rows, _ = matrix_ref.shape
    for s in range(supers):
        for q in range(rows // block):
            at = pl.multiple_of(target_ref[s, q] * block, block)
            total_ref[pl.ds(at, block), :] += dot(matrix_ref[s, q * block : (q + 1) * block, :], full_ref[s])
    part = total_ref.shape[0] // layers
    for mask in range(layers):
        at = pl.multiple_of((me_ref[0] ^ mask) * part, part)
        outs[mask][...] = total_ref[pl.ds(at, part), :].astype(outs[mask].dtype)


def add(left_ref, right_ref, out_ref):
    out_ref[...] = (left_ref[...].astype(F32) + right_ref[...].astype(F32)).astype(out_ref.dtype)


def reduce_anc(rhs_ref, left_ref, right_ref, out_ref):
    out_ref[...] = (rhs_ref[...] - (left_ref[...].astype(F32) + right_ref[...].astype(F32))).astype(BF16)


def solve_anc(size, me_ref, matrix_ref, *refs):
    blocks, (out_ref, full_ref) = refs[:size], refs[size:]
    place(me_ref, blocks, full_ref, blocks[0].shape[0])
    out_ref[...] = dot(matrix_ref[...], full_ref[...]).astype(BF16)


def finish(size, count, me_ref, matrix_ref, rhs_ref, *refs):
    blocks, parts, (out_ref, full_ref) = refs[:size], refs[size : size + count], refs[size + count :]
    place(me_ref, blocks, full_ref, blocks[0].shape[0])
    high = parts[0][...].astype(F32)
    for part in parts[1:]:
        high = high + part[...].astype(F32)
    out_ref[...] = rhs_ref[...] - high - dot(matrix_ref[...], full_ref[...])


def on_device(
    rows_n,
    layers_n,
    rhs_local,
    dinv_local,
    lower_anc,
    lower_high,
    row_blocks,
    rhs_anc,
    rhs_high,
    dinv_anc,
    lower_anc_high,
):
    rhs_mine, blocks_mine = rhs_local[0], row_blocks[0]
    me_row = lax.axis_index("row").astype(jnp.int32).reshape(1)
    me_layer = lax.axis_index("layer").astype(jnp.int32).reshape(1)
    shape = jax.ShapeDtypeStruct

    weights = tuple(
        pltpu.with_memory_space_constraint(w, pltpu.HBM)
        for w in (dinv_local[0], lower_anc[0], lower_high[0], rhs_mine, dinv_anc, lower_anc_high, rhs_anc, rhs_high)
    )
    dinv_mine, anc_mine, high_mine, rhs_own, dinv_anc, lower_anc_high, rhs_anc, rhs_high = call(
        functools.partial(stage, len(weights)),
        [shape(w.shape, w.dtype) for w in weights],
        weights,
        scratch=[pltpu.SemaphoreType.DMA((len(weights),))],
        spec=HBM,
    )
    supers, order, width = rhs_mine.shape[0], dinv_mine.shape[2], rhs_mine.shape[2]
    block = high_mine.shape[1] // blocks_mine.shape[1]
    held = rhs_high.shape[0]
    full = (supers, order, width)

    rhs_blocks = gather_row(rhs_mine, rows_n, dinv_mine)
    sol_mine = call(
        functools.partial(solve_local, rows_n),
        shape(rhs_mine.shape, BF16),
        (dinv_mine, rhs_own, *rhs_blocks[1:]),
        (me_row,),
        [pltpu.VMEM(full, BF16)],
        2 * dinv_mine.size * width,
    )
    sol_blocks = gather_row(sol_mine, rows_n)
    anc_sum, sol_full = call(
        functools.partial(reach_anc, rows_n),
        (shape((anc_mine.shape[1], width), BF16), shape(full, BF16)),
        (anc_mine, *sol_blocks),
        (me_row,),
        flops=2 * anc_mine.size * width,
    )
    high_parts = call(
        functools.partial(reach_high, layers_n, block),
        [shape((held, width), BF16)] * layers_n,
        (high_mine, sol_full),
        (me_layer, blocks_mine),
        [pltpu.VMEM((held * layers_n, width), F32)],
        2 * high_mine.size * width,
    )
    far = {mask: swap(high_parts[mask + 1], "layer", layers_n, 1) for mask in range(2, layers_n, 2)}
    near = swap(high_parts[1], "layer", layers_n, 1)

    mask = 1
    while mask < layers_n:
        other = swap(anc_sum, "layer", layers_n, mask)
        mask *= 2
        if mask < layers_n:
            anc_sum = call(add, shape(anc_sum.shape, BF16), (anc_sum, other), after=high_parts[:1])
    anc_rhs = call(reduce_anc, shape(rhs_anc.shape, BF16), (rhs_anc, anc_sum, other))
    received = [near]
    for mask, other in far.items():
        both = call(add, shape(other.shape, BF16), (high_parts[mask], other))
        received.append(swap(both, "layer", layers_n, mask))

    anc_solved = call(
        functools.partial(solve_anc, rows_n),
        shape(rhs_anc.shape, BF16),
        (dinv_anc, *gather_row(anc_rhs, rows_n)),
        (me_row,),
        [pltpu.VMEM((dinv_anc.shape[1], width), BF16)],
        2 * dinv_anc.size * width,
    )
    anc_blocks = gather_row(anc_solved, rows_n)
    sol_out, anc_out = call(
        functools.partial(emit, 2),
        [shape(sol_mine.shape, BF16), shape(anc_solved.shape, BF16)],
        (sol_mine, anc_solved),
    )
    high_new = call(
        functools.partial(finish, rows_n, 1 + len(received)),
        shape(rhs_high.shape, F32),
        (lower_anc_high, rhs_high, *anc_blocks, high_parts[0], *received),
        (me_row,),
        [pltpu.VMEM((lower_anc_high.shape[1], width), BF16)],
        2 * lower_anc_high.size * width,
    )
    return (sol_out[None], anc_out, high_new)


def solution(mesh):
    return jax.shard_map(
        functools.partial(on_device, mesh.shape["row"], mesh.shape["layer"]),
        mesh=mesh,
        in_specs=(
            P("layer", None, "row", None),
            P("layer", None, "row", None),
            P("layer", None, "row", None),
            P("layer", None, "row", None),
            P("layer", None, "row"),
            P("row", None),
            P(("row", "layer"), None),
            P("row", None),
            P(("row", "layer"), None),
        ),
        out_specs=(P("layer", None, "row", None), P("row", None), P(("row", "layer"), None)),
        check_vma=False,
    )
```

```python
import functools

import jax
import jax.numpy as jnp
from jax import lax
from jax.experimental import pallas as pl
from jax.experimental.pallas import tpu as pltpu
from jax.sharding import PartitionSpec as P

F32 = jnp.float32
BF16 = jnp.bfloat16
VMEM = pl.BlockSpec(memory_space=pltpu.VMEM)
SMEM = pl.BlockSpec(memory_space=pltpu.SMEM)
ANY = pl.BlockSpec(memory_space=pl.ANY)
HBM = pl.BlockSpec(memory_space=pltpu.HBM)


def swap(value, axis, size, mask):
    return lax.ppermute(value, axis, [(i, i ^ mask) for i in range(size)])


def gather_row(value, size, after=None):
    blocks = {0: value}
    for mask in range(2, size, 2):
        blocks[mask] = swap(value, "row", size, mask)
    blocks[1] = swap(value, "row", size, 1)
    for mask in range(2, size, 2):
        if after is not None:
            blocks[mask], _ = lax.optimization_barrier((blocks[mask], after))
        blocks[mask + 1] = swap(blocks[mask], "row", size, 1)
    return [blocks[mask] for mask in range(size)]


def call(body, outs, operands, scalars=(), scratch=(), flops=0, after=(), specs=None, limit=16):
    count, waits = len(scalars) + len(operands), len(after)

    def kernel(*refs):
        body(*refs[:count], *refs[count + waits :])

    moved = sum(o.size * o.dtype.itemsize for o in operands)
    return pl.pallas_call(
        kernel,
        out_shape=outs,
        in_specs=[SMEM] * len(scalars) + (specs or [VMEM] * len(operands)) + [ANY] * waits,
        out_specs=jax.tree.map(lambda _: VMEM, outs),
        scratch_shapes=list(scratch),
        cost_estimate=pl.CostEstimate(flops=flops, bytes_accessed=moved, transcendentals=0),
        compiler_params=pltpu.CompilerParams(vmem_limit_bytes=limit * 1024 * 1024),
    )(*scalars, *operands, *after)


def stage(count, *refs):
    sems = refs[2 * count]
    copies = [pltpu.make_async_copy(refs[i], refs[count + i], sems.at[i]) for i in range(count)]
    for copy in copies:
        copy.start()
    for copy in copies:
        copy.wait()


def place(me_ref, blocks, full_ref, rows):
    for mask, block in enumerate(blocks):
        at = pl.multiple_of((me_ref[0] ^ mask) * rows, rows)
        if len(full_ref.shape) == 3:
            full_ref[:, pl.ds(at, rows), :] = block[...]
        else:
            full_ref[pl.ds(at, rows), :] = block[...]


def dot(left, right):
    return jnp.dot(left, right, preferred_element_type=F32)


def solve_local(size, me_ref, matrix_ref, *refs):
    blocks, (out_ref, full_ref) = refs[:size], refs[size:]
    place(me_ref, blocks, full_ref, blocks[0].shape[1])
    for s in range(matrix_ref.shape[0]):
        out_ref[s] = dot(matrix_ref[s], full_ref[s]).astype(BF16)


def reach(size, layers, block, me_row, me_layer, target_ref, anc_ref, high_ref, *refs):
    blocks, refs = refs[:size], refs[size:]
    anc_out, outs, (full_ref, matrix_ref, total_ref, sems) = refs[0], refs[1:-4], refs[-4:]
    supers, rows, _ = high_ref.shape
    copies = []
    for s in range(supers):
        for q in range(rows // block):
            at = pl.ds(q * block, block)
            copies.append(
                pltpu.make_async_copy(high_ref.at[s, at], matrix_ref.at[s, at], sems.at[s * (rows // block) + q])
            )
            copies[-1].start()
    place(me_row, blocks, full_ref, blocks[0].shape[1])
    anc = dot(anc_ref[0], full_ref[0])
    for s in range(1, supers):
        anc = anc + dot(anc_ref[s], full_ref[s])
    anc_out[...] = anc.astype(BF16)
    total_ref[...] = jnp.zeros_like(total_ref)
    for s in range(supers):
        for q in range(rows // block):
            copies[s * (rows // block) + q].wait()
            at = pl.multiple_of(target_ref[s, q] * block, block)
            total_ref[pl.ds(at, block), :] += dot(matrix_ref[s, q * block : (q + 1) * block, :], full_ref[s])
    part = total_ref.shape[0] // layers
    for mask in range(layers):
        at = pl.multiple_of((me_layer[0] ^ mask) * part, part)
        outs[mask][...] = total_ref[pl.ds(at, part), :].astype(outs[mask].dtype)


def add(left_ref, right_ref, out_ref):
    out_ref[...] = (left_ref[...].astype(F32) + right_ref[...].astype(F32)).astype(out_ref.dtype)


def reduce_anc(rhs_ref, left_ref, right_ref, out_ref):
    out_ref[...] = (rhs_ref[...] - (left_ref[...].astype(F32) + right_ref[...].astype(F32))).astype(BF16)


def solve_anc(size, me_row, sol_ref, *refs):
    blocks, refs = refs[:size], refs[size:]
    matrices, (reach_ref, rhs_ref) = refs[:size], refs[size : size + 2]
    sol_out, anc_out, base_out, full_ref, solved_ref, matrix_ref, reach_buf, rhs_buf, sems = refs[size + 2 :]
    rows = blocks[0].shape[0]
    copies = [pltpu.make_async_copy(matrices[i], matrix_ref.at[i], sems.at[i]) for i in range(size)]
    copies.append(pltpu.make_async_copy(reach_ref, reach_buf, sems.at[size]))
    copies.append(pltpu.make_async_copy(rhs_ref, rhs_buf, sems.at[size + 1]))
    for copy in copies:
        copy.start()
    sol_out[...] = sol_ref[...]
    place(me_row, blocks, full_ref, rows)
    for mask in range(size):
        copies[mask].wait()
        at = pl.multiple_of((me_row[0] ^ mask) * rows, rows)
        solved = dot(matrix_ref[mask], full_ref[...]).astype(BF16)
        solved_ref[pl.ds(at, rows), :] = solved
        if mask == 0:
            anc_out[...] = solved
    copies[size].wait()
    copies[size + 1].wait()
    base_out[...] = rhs_buf[...] - dot(reach_buf[...], solved_ref[...])


def sum_high(own_ref, *refs):
    parts, (out_ref, mark_ref) = refs[:-2], refs[-2:]
    total = own_ref[...]
    for part in parts:
        total = total + part[...].astype(F32)
    out_ref[...] = total
    mark_ref[...] = total[: mark_ref.shape[0], : mark_ref.shape[1]].astype(BF16)


def finish(base_ref, sum_ref, out_ref):
    out_ref[...] = base_ref[...] - sum_ref[...]


def on_device(
    rows_n,
    layers_n,
    rhs_local,
    dinv_local,
    lower_anc,
    lower_high,
    row_blocks,
    rhs_anc,
    rhs_high,
    dinv_anc,
    lower_anc_high,
):
    rhs_mine, blocks_mine = rhs_local[0], row_blocks[0]
    me_row = lax.axis_index("row").astype(jnp.int32).reshape(1)
    me_layer = lax.axis_index("layer").astype(jnp.int32).reshape(1)
    shape = jax.ShapeDtypeStruct

    in_hbm = lambda x: pltpu.with_memory_space_constraint(x, pltpu.HBM)
    weights = [in_hbm(w) for w in (dinv_local[0], lower_anc[0], rhs_mine, rhs_anc)]
    dinv_mine, anc_mine, rhs_own, rhs_anc = call(
        functools.partial(stage, len(weights)),
        [shape(w.shape, w.dtype) for w in weights],
        weights,
        scratch=[pltpu.SemaphoreType.DMA((len(weights),))],
        specs=[HBM] * len(weights),
    )
    high_mine = lower_high[0]
    supers, order, width = rhs_mine.shape[0], dinv_mine.shape[2], rhs_mine.shape[2]
    block = high_mine.shape[1] // blocks_mine.shape[1]
    held = rhs_high.shape[0]
    full = (supers, order, width)

    rhs_blocks = gather_row(rhs_mine, rows_n, dinv_mine)
    sol_mine = call(
        functools.partial(solve_local, rows_n),
        shape(rhs_mine.shape, BF16),
        (dinv_mine, rhs_own, *rhs_blocks[1:]),
        (me_row,),
        [pltpu.VMEM(full, BF16)],
        2 * dinv_mine.size * width,
    )
    sol_blocks = gather_row(sol_mine, rows_n)
    anc_sum, own, near, *others = call(
        functools.partial(reach, rows_n, layers_n, block),
        [shape((anc_mine.shape[1], width), BF16)]
        + [shape((held, width), F32), shape((held, width), BF16)] * (layers_n // 2),
        (anc_mine, in_hbm(high_mine), *sol_blocks),
        (me_row, me_layer, blocks_mine),
        [
            pltpu.VMEM(full, BF16),
            pltpu.VMEM(high_mine.shape, BF16),
            pltpu.VMEM((held * layers_n, width), F32),
            pltpu.SemaphoreType.DMA((supers * blocks_mine.shape[1],)),
        ],
        2 * (high_mine.size + anc_mine.size) * width,
        specs=[VMEM, HBM] + [VMEM] * rows_n,
    )
    dinv_anc, _ = lax.optimization_barrier((dinv_anc, sol_blocks[-1]))
    dinv_blocks = gather_row(dinv_anc, rows_n)

    mask = 1
    while mask < layers_n:
        other = swap(anc_sum, "layer", layers_n, mask)
        mask *= 2
        if mask < layers_n:
            anc_sum = call(add, shape(anc_sum.shape, BF16), (anc_sum, other))
    anc_rhs = call(reduce_anc, shape(rhs_anc.shape, BF16), (rhs_anc, anc_sum, other), after=dinv_blocks[2::2])
    near = swap(near, "layer", layers_n, 1)
    received = []
    for mask in range(2, layers_n, 2):
        at = mask - 2
        other = swap(others[at + 1], "layer", layers_n, 1)
        both = call(add, shape(other.shape, BF16), (others[at], other))
        received.append(swap(both, "layer", layers_n, mask))

    sol_out, anc_out, base = call(
        functools.partial(solve_anc, rows_n),
        [shape(sol_mine.shape, BF16), shape(rhs_anc.shape, BF16), shape(rhs_high.shape, F32)],
        (sol_mine, *gather_row(anc_rhs, rows_n), *dinv_blocks, lower_anc_high, rhs_high),
        (me_row,),
        [
            pltpu.VMEM((dinv_anc.shape[1], width), BF16),
            pltpu.VMEM((dinv_anc.shape[1], width), BF16),
            pltpu.VMEM((rows_n, *dinv_anc.shape), BF16),
            pltpu.VMEM(lower_anc_high.shape, BF16),
            pltpu.VMEM(rhs_high.shape, F32),
            pltpu.SemaphoreType.DMA((rows_n + 2,)),
        ],
        2 * (lower_anc_high.size + dinv_anc.size * rows_n) * width,
        specs=[VMEM] * (1 + rows_n) + [ANY] * (rows_n + 2),
    )
    high_sum, mark = call(
        sum_high, [shape(rhs_high.shape, F32), shape((16, 128), BF16)], (own, near, *received)
    )
    for _ in range(2):
        mark = swap(mark, "row", rows_n, 1)
    high_new = call(finish, shape(rhs_high.shape, F32), (base, high_sum), after=(mark,))
    return (sol_out[None], anc_out, high_new)


def solution(mesh):
    return jax.shard_map(
        functools.partial(on_device, mesh.shape["row"], mesh.shape["layer"]),
        mesh=mesh,
        in_specs=(
            P("layer", None, "row", None),
            P("layer", None, "row", None),
            P("layer", None, "row", None),
            P("layer", None, "row", None),
            P("layer", None, "row"),
            P("row", None),
            P(("row", "layer"), None),
            P("row", None),
            P(("row", "layer"), None),
        ),
        out_specs=(P("layer", None, "row", None), P("row", None), P(("row", "layer"), None)),
        check_vma=False,
    )
```

```python
import functools

import jax
import jax.numpy as jnp
from jax import lax
from jax.experimental import pallas as pl
from jax.experimental.pallas import tpu as pltpu
from jax.sharding import PartitionSpec as P

F32 = jnp.float32
BF16 = jnp.bfloat16
VMEM = pl.BlockSpec(memory_space=pltpu.VMEM)
SMEM = pl.BlockSpec(memory_space=pltpu.SMEM)
ANY = pl.BlockSpec(memory_space=pl.ANY)
HBM = pl.BlockSpec(memory_space=pltpu.HBM)
CHUNKS = 2


def swap(value, axis, size, mask):
    return lax.ppermute(value, axis, [(i, i ^ mask) for i in range(size)])


def gather_row(value, size, after=None):
    blocks = {0: value}
    for mask in range(2, size, 2):
        blocks[mask] = swap(value, "row", size, mask)
    blocks[1] = swap(value, "row", size, 1)
    for mask in range(2, size, 2):
        if after is not None:
            blocks[mask], _ = lax.optimization_barrier((blocks[mask], after))
        blocks[mask + 1] = swap(blocks[mask], "row", size, 1)
    return [blocks[mask] for mask in range(size)]


def call(body, outs, operands, scalars=(), scratch=(), flops=0, after=(), specs=None, limit=16):
    count, waits = len(scalars) + len(operands), len(after)

    def kernel(*refs):
        body(*refs[:count], *refs[count + waits :])

    moved = sum(o.size * o.dtype.itemsize for o in operands)
    return pl.pallas_call(
        kernel,
        out_shape=outs,
        in_specs=[SMEM] * len(scalars) + (specs or [VMEM] * len(operands)) + [ANY] * waits,
        out_specs=jax.tree.map(lambda _: VMEM, outs),
        scratch_shapes=list(scratch),
        cost_estimate=pl.CostEstimate(flops=flops, bytes_accessed=moved, transcendentals=0),
        compiler_params=pltpu.CompilerParams(vmem_limit_bytes=limit * 1024 * 1024),
    )(*scalars, *operands, *after)


def stage(count, *refs):
    sems = refs[2 * count]
    copies = []
    for i in range(count):
        source = refs[i] if refs[i].shape == refs[count + i].shape else refs[i].at[0]
        copies.append(pltpu.make_async_copy(source, refs[count + i], sems.at[i]))
    for copy in copies:
        copy.start()
    for copy in copies:
        copy.wait()


def place(me_ref, blocks, full_ref, rows):
    for mask, block in enumerate(blocks):
        at = pl.multiple_of((me_ref[0] ^ mask) * rows, rows)
        if len(full_ref.shape) == 3:
            full_ref[:, pl.ds(at, rows), :] = block[...]
        else:
            full_ref[pl.ds(at, rows), :] = block[...]


def dot(left, right):
    return jnp.dot(left, right, preferred_element_type=F32)


def solve_local(size, me_ref, matrix_ref, *refs):
    blocks, (out_ref, full_ref) = refs[:size], refs[size:]
    place(me_ref, blocks, full_ref, blocks[0].shape[1])
    for s in range(matrix_ref.shape[0]):
        out_ref[s] = dot(matrix_ref[s], full_ref[s]).astype(BF16)


def reach_anc(size, me_row, matrix_ref, *refs):
    blocks, (out_ref, full_ref) = refs[:size], refs[size:]
    place(me_row, blocks, full_ref, blocks[0].shape[1])
    total = dot(matrix_ref[0], full_ref[0])
    for s in range(1, matrix_ref.shape[0]):
        total = total + dot(matrix_ref[s], full_ref[s])
    out_ref[...] = total.astype(BF16)


def reach_high(layers, block, me_layer, target_ref, full_ref, first_ref, high_ref, *refs):
    outs, (matrix_ref, total_ref, sems) = refs[:-3], refs[-3:]
    supers, rows, _ = high_ref.shape
    copies = [pltpu.make_async_copy(high_ref.at[s], matrix_ref.at[s - 1], sems.at[s - 1]) for s in range(1, supers)]
    for copy in copies:
        copy.start()
    total_ref[...] = jnp.zeros_like(total_ref)
    for s in range(supers):
        if s:
            copies[s - 1].wait()
        product = dot(matrix_ref[s - 1] if s else first_ref[...], full_ref[s])
        for q in range(rows // block):
            at = pl.multiple_of(target_ref[s, q] * block, block)
            total_ref[pl.ds(at, block), :] += product[q * block : (q + 1) * block, :]
    part = total_ref.shape[0] // layers
    outs = list(outs)
    for mask in range(layers):
        start = (me_layer[0] ^ mask) * part
        rows = outs[0].shape[0]
        for piece in range(part // rows):
            out = outs.pop(0)
            at = pl.multiple_of(start + piece * rows, rows)
            out[...] = total_ref[pl.ds(at, rows), :].astype(out.dtype)


def add(kept_ref, *refs):
    out_ref, rows = refs[-1], refs[0].shape[0]
    for i, ref in enumerate(refs[:-1]):
        at = pl.ds(i * rows, rows)
        out_ref[at, :] = (kept_ref[at, :].astype(F32) + ref[...].astype(F32)).astype(out_ref.dtype)


def reduce_anc(rhs_ref, left_ref, right_ref, out_ref):
    out_ref[...] = (rhs_ref[...] - (left_ref[...].astype(F32) + right_ref[...].astype(F32))).astype(BF16)


def solve_anc(size, me_row, matrix_ref, *refs):
    blocks, (sol_out, full_ref) = refs[:size], refs[size:]
    place(me_row, blocks, full_ref, blocks[0].shape[0])
    sol_out[...] = dot(matrix_ref[...], full_ref[...]).astype(BF16)


def finish(size, me_row, sol_ref, rhs_ref, own_ref, matrix_ref, *refs):
    blocks, parts, (sol_out, anc_out, high_out, full_ref) = refs[:size], refs[size:-4], refs[-4:]
    sol_out[...] = sol_ref[...]
    anc_out[...] = blocks[0][...]
    place(me_row, blocks, full_ref, blocks[0].shape[0])
    high = own_ref[...]
    for part in parts:
        high = high + part[...].astype(F32)
    high_out[...] = rhs_ref[...] - high - dot(matrix_ref[...], full_ref[...])


def on_device(
    rows_n,
    layers_n,
    rhs_local,
    dinv_local,
    lower_anc,
    lower_high,
    row_blocks,
    rhs_anc,
    rhs_high,
    dinv_anc,
    lower_anc_high,
):
    rhs_mine, blocks_mine = rhs_local[0], row_blocks[0]
    me_row = lax.axis_index("row").astype(jnp.int32).reshape(1)
    me_layer = lax.axis_index("layer").astype(jnp.int32).reshape(1)
    shape = jax.ShapeDtypeStruct

    in_hbm = lambda x: pltpu.with_memory_space_constraint(x, pltpu.HBM)
    weights = [in_hbm(w) for w in (dinv_local[0], lower_anc[0], rhs_mine, rhs_anc)]
    dinv_mine, anc_mine, rhs_own, rhs_anc = call(
        functools.partial(stage, len(weights)),
        [shape(w.shape, w.dtype) for w in weights],
        weights,
        scratch=[pltpu.SemaphoreType.DMA((len(weights),))],
        specs=[HBM] * len(weights),
    )
    high_mine = lower_high[0]
    supers, order, width = rhs_mine.shape[0], dinv_mine.shape[2], rhs_mine.shape[2]
    block = high_mine.shape[1] // blocks_mine.shape[1]
    held = rhs_high.shape[0]
    full = (supers, order, width)

    rhs_blocks = gather_row(rhs_mine, rows_n, dinv_mine)
    sol_mine = call(
        functools.partial(solve_local, rows_n),
        shape(rhs_mine.shape, BF16),
        (dinv_mine, rhs_own, *rhs_blocks[1:]),
        (me_row,),
        [pltpu.VMEM(full, BF16)],
        2 * dinv_mine.size * width,
    )
    high_first, = call(
        functools.partial(stage, 1),
        [shape(high_mine.shape[1:], BF16)],
        [in_hbm(high_mine)],
        scratch=[pltpu.SemaphoreType.DMA((1,))],
        specs=[HBM],
        after=(sol_mine,),
    )
    sol_blocks = gather_row(sol_mine, rows_n, high_first)
    anc_sum, sol_full = call(
        functools.partial(reach_anc, rows_n),
        (shape((anc_mine.shape[1], width), BF16), shape(full, BF16)),
        (anc_mine, *sol_blocks),
        (me_row,),
        flops=2 * anc_mine.size * width,
    )
    kept, sent = [shape((held, width), F32)], [shape((held, width), BF16)]
    pieces = [shape((held // CHUNKS, width), BF16)] * CHUNKS
    own, near, *others = call(
        functools.partial(reach_high, layers_n, block),
        kept + sent + (kept + pieces) * (layers_n // 2 - 1),
        (sol_full, high_first, in_hbm(high_mine)),
        (me_layer, blocks_mine),
        [
            pltpu.VMEM((supers - 1, *high_mine.shape[1:]), BF16),
            pltpu.VMEM((held * layers_n, width), F32),
            pltpu.SemaphoreType.DMA((supers - 1,)),
        ],
        2 * high_mine.size * width,
        specs=[VMEM, VMEM, HBM],
    )
    mask = 1
    while mask < layers_n:
        other = swap(anc_sum, "layer", layers_n, mask)
        mask *= 2
        if mask < layers_n:
            anc_sum = call(add, shape(anc_sum.shape, BF16), (anc_sum, other))
    anc_rhs = call(reduce_anc, shape(rhs_anc.shape, BF16), (rhs_anc, anc_sum, other))
    received = [swap(near, "layer", layers_n, 1)]
    for mask in range(2, layers_n, 2):
        mine, *far = others[: 1 + CHUNKS]
        others = others[1 + CHUNKS :]
        far = [swap(piece, "layer", layers_n, 1) for piece in far]
        received.append(swap(call(add, sent[0], (mine, *far)), "layer", layers_n, mask))

    anc_solved = call(
        functools.partial(solve_anc, rows_n),
        shape(rhs_anc.shape, BF16),
        (dinv_anc, *gather_row(anc_rhs, rows_n)),
        (me_row,),
        [pltpu.VMEM((order, width), BF16)],
        2 * dinv_anc.size * width,
    )
    sol_out, anc_out, high_new = call(
        functools.partial(finish, rows_n),
        [shape(sol_mine.shape, BF16), shape(rhs_anc.shape, BF16), shape(rhs_high.shape, F32)],
        (sol_mine, rhs_high, own, lower_anc_high, *gather_row(anc_solved, rows_n), *received),
        (me_row,),
        [pltpu.VMEM((order, width), BF16)],
        2 * lower_anc_high.size * width,
    )
    return (sol_out[None], anc_out, high_new)


def solution(mesh):
    return jax.shard_map(
        functools.partial(on_device, mesh.shape["row"], mesh.shape["layer"]),
        mesh=mesh,
        in_specs=(
            P("layer", None, "row", None),
            P("layer", None, "row", None),
            P("layer", None, "row", None),
            P("layer", None, "row", None),
            P("layer", None, "row"),
            P("row", None),
            P(("row", "layer"), None),
            P("row", None),
            P(("row", "layer"), None),
        ),
        out_specs=(P("layer", None, "row", None), P("row", None), P(("row", "layer"), None)),
        check_vma=False,
    )
```

```python
import functools

import jax
import jax.numpy as jnp
from jax import lax
from jax.experimental import pallas as pl
from jax.experimental.pallas import tpu as pltpu
from jax.sharding import PartitionSpec as P

F32 = jnp.float32
BF16 = jnp.bfloat16
VMEM = pl.BlockSpec(memory_space=pltpu.VMEM)
SMEM = pl.BlockSpec(memory_space=pltpu.SMEM)
ANY = pl.BlockSpec(memory_space=pl.ANY)
HBM = pl.BlockSpec(memory_space=pltpu.HBM)
CHUNKS = 2


def swap(value, axis, size, mask):
    return lax.ppermute(value, axis, [(i, i ^ mask) for i in range(size)])


def gather_row(value, size, after=None):
    blocks = {0: value}
    for mask in range(2, size, 2):
        blocks[mask] = swap(value, "row", size, mask)
    blocks[1] = swap(value, "row", size, 1)
    for mask in range(2, size, 2):
        if after is not None and mask == 2:
            blocks[mask], _ = lax.optimization_barrier((blocks[mask], after))
        blocks[mask + 1] = swap(blocks[mask], "row", size, 1)
    return [blocks[mask] for mask in reversed(range(size))]


def call(body, outs, operands, scalars=(), scratch=(), flops=0, after=(), specs=None, limit=16):
    count, waits = len(scalars) + len(operands), len(after)

    def kernel(*refs):
        body(*refs[:count], *refs[count + waits :])

    moved = sum(o.size * o.dtype.itemsize for o in operands)
    return pl.pallas_call(
        kernel,
        out_shape=outs,
        in_specs=[SMEM] * len(scalars) + (specs or [VMEM] * len(operands)) + [ANY] * waits,
        out_specs=jax.tree.map(lambda _: VMEM, outs),
        scratch_shapes=list(scratch),
        cost_estimate=pl.CostEstimate(flops=flops, bytes_accessed=moved, transcendentals=0),
        compiler_params=pltpu.CompilerParams(vmem_limit_bytes=limit * 1024 * 1024),
    )(*scalars, *operands, *after)


def stage(count, *refs):
    sems = refs[2 * count]
    copies = []
    for i in range(count):
        source = refs[i] if refs[i].shape == refs[count + i].shape else refs[i].at[0]
        copies.append(pltpu.make_async_copy(source, refs[count + i], sems.at[i]))
    for copy in copies:
        copy.start()
    for copy in copies:
        copy.wait()


def stage_late(count, own_ref, high_ref, *refs):
    outs, (base_ref, high_buf, sems) = refs[count : 2 * count], refs[2 * count :]
    copies = [pltpu.make_async_copy(high_ref, high_buf, sems.at[count])]
    copies += [pltpu.make_async_copy(refs[i], outs[i], sems.at[i]) for i in range(count)]
    for copy in copies:
        copy.start()
    copies[0].wait()
    base_ref[...] = high_buf[...] - own_ref[...]
    for copy in copies[1:]:
        copy.wait()


def place(me_ref, blocks, full_ref, rows):
    for mask, block in enumerate(blocks[::-1]):
        at = pl.multiple_of((me_ref[0] ^ mask) * rows, rows)
        if len(full_ref.shape) == 3:
            full_ref[:, pl.ds(at, rows), :] = block[...]
        else:
            full_ref[pl.ds(at, rows), :] = block[...]


def dot(left, right):
    return jnp.dot(left, right, preferred_element_type=F32)


def solve_local(size, me_ref, matrix_ref, *refs):
    blocks, (out_ref, full_ref) = refs[:size], refs[size:]
    place(me_ref, blocks, full_ref, blocks[0].shape[1])
    for s in range(matrix_ref.shape[0]):
        out_ref[s] = dot(matrix_ref[s], full_ref[s]).astype(BF16)


def reach_anc(size, me_row, matrix_ref, *refs):
    blocks, (out_ref, full_ref) = refs[:size], refs[size:]
    place(me_row, blocks, full_ref, blocks[0].shape[1])
    total = dot(matrix_ref[0], full_ref[0])
    for s in range(1, matrix_ref.shape[0]):
        total = total + dot(matrix_ref[s], full_ref[s])
    out_ref[...] = total.astype(BF16)


def reach_high(layers, block, me_layer, target_ref, full_ref, first_ref, high_ref, *refs):
    outs, (matrix_ref, total_ref, sems) = refs[:-3], refs[-3:]
    supers, rows, _ = high_ref.shape
    copies = [pltpu.make_async_copy(high_ref.at[s], matrix_ref.at[s - 1], sems.at[s - 1]) for s in range(1, supers)]
    for copy in copies:
        copy.start()
    total_ref[...] = jnp.zeros_like(total_ref)
    for s in range(supers):
        if s:
            copies[s - 1].wait()
        product = dot(matrix_ref[s - 1] if s else first_ref[...], full_ref[s])
        for q in range(rows // block):
            at = pl.multiple_of(target_ref[s, q] * block, block)
            total_ref[pl.ds(at, block), :] += product[q * block : (q + 1) * block, :]
    part = total_ref.shape[0] // layers
    outs = list(outs)
    for mask in range(layers):
        start = (me_layer[0] ^ mask) * part
        rows = outs[0].shape[0]
        for piece in range(part // rows):
            out = outs.pop(0)
            at = pl.multiple_of(start + piece * rows, rows)
            out[...] = total_ref[pl.ds(at, rows), :].astype(out.dtype)


def add(kept_ref, *refs):
    out_ref, rows = refs[-1], refs[0].shape[0]
    for i, ref in enumerate(refs[:-1]):
        at = pl.ds(i * rows, rows)
        out_ref[at, :] = (kept_ref[at, :].astype(F32) + ref[...].astype(F32)).astype(out_ref.dtype)


def reduce_anc(rhs_ref, left_ref, right_ref, out_ref):
    out_ref[...] = (rhs_ref[...] - (left_ref[...].astype(F32) + right_ref[...].astype(F32))).astype(BF16)


def solve_anc(size, me_row, matrix_ref, *refs):
    blocks, (sol_out, full_ref) = refs[:size], refs[size:]
    place(me_row, blocks, full_ref, blocks[0].shape[0])
    sol_out[...] = dot(matrix_ref[...], full_ref[...]).astype(BF16)


def finish(size, me_row, sol_ref, base_ref, matrix_ref, *refs):
    blocks, parts, (sol_out, anc_out, high_out, full_ref) = refs[:size], refs[size:-4], refs[-4:]
    sol_out[...] = sol_ref[...]
    anc_out[...] = blocks[-1][...]
    place(me_row, blocks, full_ref, blocks[0].shape[0])
    high = parts[0][...].astype(F32)
    for part in parts[1:]:
        high = high + part[...].astype(F32)
    high_out[...] = base_ref[...] - high - dot(matrix_ref[...], full_ref[...])


def on_device(
    rows_n,
    layers_n,
    rhs_local,
    dinv_local,
    lower_anc,
    lower_high,
    row_blocks,
    rhs_anc,
    rhs_high,
    dinv_anc,
    lower_anc_high,
):
    rhs_mine, blocks_mine = rhs_local[0], row_blocks[0]
    me_row = lax.axis_index("row").astype(jnp.int32).reshape(1)
    me_layer = lax.axis_index("layer").astype(jnp.int32).reshape(1)
    shape = jax.ShapeDtypeStruct

    in_hbm = lambda x: pltpu.with_memory_space_constraint(x, pltpu.HBM)
    weights = [in_hbm(w) for w in (dinv_local[0], lower_anc[0], rhs_mine)]
    dinv_mine, anc_mine, rhs_own = call(
        functools.partial(stage, len(weights)),
        [shape(w.shape, w.dtype) for w in weights],
        weights,
        scratch=[pltpu.SemaphoreType.DMA((len(weights),))],
        specs=[HBM] * len(weights),
    )
    high_mine = lower_high[0]
    supers, order, width = rhs_mine.shape[0], dinv_mine.shape[2], rhs_mine.shape[2]
    block = high_mine.shape[1] // blocks_mine.shape[1]
    held = rhs_high.shape[0]
    full = (supers, order, width)

    rhs_blocks = gather_row(rhs_mine, rows_n, dinv_mine)
    sol_mine = call(
        functools.partial(solve_local, rows_n),
        shape(rhs_mine.shape, BF16),
        (dinv_mine, *rhs_blocks[:-1], rhs_own),
        (me_row,),
        [pltpu.VMEM(full, BF16)],
        2 * dinv_mine.size * width,
    )
    high_first, = call(
        functools.partial(stage, 1),
        [shape(high_mine.shape[1:], BF16)],
        [in_hbm(high_mine)],
        scratch=[pltpu.SemaphoreType.DMA((1,))],
        specs=[HBM],
        after=(sol_mine,),
    )
    sol_blocks = gather_row(sol_mine, rows_n, high_first)
    anc_sum, sol_full = call(
        functools.partial(reach_anc, rows_n),
        (shape((anc_mine.shape[1], width), BF16), shape(full, BF16)),
        (anc_mine, *sol_blocks),
        (me_row,),
        flops=2 * anc_mine.size * width,
    )
    kept, sent = [shape((held, width), F32)], [shape((held, width), BF16)]
    pieces = [shape((held // CHUNKS, width), BF16)] * CHUNKS
    own, near, *others = call(
        functools.partial(reach_high, layers_n, block),
        kept + sent + (kept + pieces) * (layers_n // 2 - 1),
        (sol_full, high_first, in_hbm(high_mine)),
        (me_layer, blocks_mine),
        [
            pltpu.VMEM((supers - 1, *high_mine.shape[1:]), BF16),
            pltpu.VMEM((held * layers_n, width), F32),
            pltpu.SemaphoreType.DMA((supers - 1,)),
        ],
        2 * high_mine.size * width,
        specs=[VMEM, VMEM, HBM],
    )
    mask = 1
    while mask < layers_n:
        other = swap(anc_sum, "layer", layers_n, mask)
        mask *= 2
        if mask < layers_n:
            anc_sum = call(add, shape(anc_sum.shape, BF16), (anc_sum, other))
    late = [in_hbm(w) for w in (rhs_anc, dinv_anc, lower_anc_high)]
    rhs_anc, dinv_anc, lower_anc_high, base = call(
        functools.partial(stage_late, len(late)),
        [shape(w.shape, w.dtype) for w in late] + [shape(rhs_high.shape, F32)],
        [own, in_hbm(rhs_high), *late],
        scratch=[pltpu.VMEM(rhs_high.shape, F32), pltpu.SemaphoreType.DMA((len(late) + 1,))],
        specs=[VMEM] + [HBM] * (1 + len(late)),
    )
    anc_rhs = call(reduce_anc, shape(rhs_anc.shape, BF16), (rhs_anc, anc_sum, other))
    received = []
    for mask in range(2, layers_n, 2):
        mine, *far = others[: 1 + CHUNKS]
        others = others[1 + CHUNKS :]
        far = [swap(piece, "layer", layers_n, 1) for piece in far]
        received.append(swap(call(add, sent[0], (mine, *far)), "layer", layers_n, mask))

    anc_solved = call(
        functools.partial(solve_anc, rows_n),
        shape(rhs_anc.shape, BF16),
        (dinv_anc, *gather_row(anc_rhs, rows_n)),
        (me_row,),
        [pltpu.VMEM((order, width), BF16)],
        2 * dinv_anc.size * width,
    )
    near, anc_solved = lax.optimization_barrier((near, anc_solved))
    received.append(swap(near, "layer", layers_n, 1))
    sol_out, anc_out, high_new = call(
        functools.partial(finish, rows_n),
        [shape(sol_mine.shape, BF16), shape(rhs_anc.shape, BF16), shape(rhs_high.shape, F32)],
        (sol_mine, base, lower_anc_high, *gather_row(anc_solved, rows_n), *received),
        (me_row,),
        [pltpu.VMEM((order, width), BF16)],
        2 * lower_anc_high.size * width,
    )
    return (sol_out[None], anc_out, high_new)


def solution(mesh):
    return jax.shard_map(
        functools.partial(on_device, mesh.shape["row"], mesh.shape["layer"]),
        mesh=mesh,
        in_specs=(
            P("layer", None, "row", None),
            P("layer", None, "row", None),
            P("layer", None, "row", None),
            P("layer", None, "row", None),
            P("layer", None, "row"),
            P("row", None),
            P(("row", "layer"), None),
            P("row", None),
            P(("row", "layer"), None),
        ),
        out_specs=(P("layer", None, "row", None), P("row", None), P(("row", "layer"), None)),
        check_vma=False,
    )
```

```python
import functools

import jax
import jax.numpy as jnp
from jax import lax
from jax.experimental import pallas as pl
from jax.experimental.pallas import tpu as pltpu
from jax.sharding import PartitionSpec as P

F32 = jnp.float32
BF16 = jnp.bfloat16
VMEM = pl.BlockSpec(memory_space=pltpu.VMEM)
SMEM = pl.BlockSpec(memory_space=pltpu.SMEM)
ANY = pl.BlockSpec(memory_space=pl.ANY)
HBM = pl.BlockSpec(memory_space=pltpu.HBM)
CHUNKS = 2


def swap(value, axis, size, mask):
    return lax.ppermute(value, axis, [(i, i ^ mask) for i in range(size)])


def gather_row(value, size, after=None):
    blocks = {0: value}
    for mask in range(2, size, 2):
        blocks[mask] = swap(value, "row", size, mask)
    blocks[1] = swap(value, "row", size, 1)
    for mask in range(2, size, 2):
        if after is not None and mask == 2:
            blocks[mask], _ = lax.optimization_barrier((blocks[mask], after))
        blocks[mask + 1] = swap(blocks[mask], "row", size, 1)
    return [blocks[mask] for mask in reversed(range(size))]


def call(body, outs, operands, scalars=(), scratch=(), flops=0, after=(), specs=None, limit=16):
    count, waits = len(scalars) + len(operands), len(after)

    def kernel(*refs):
        body(*refs[:count], *refs[count + waits :])

    moved = sum(o.size * o.dtype.itemsize for o in operands)
    return pl.pallas_call(
        kernel,
        out_shape=outs,
        in_specs=[SMEM] * len(scalars) + (specs or [VMEM] * len(operands)) + [ANY] * waits,
        out_specs=jax.tree.map(lambda _: VMEM, outs),
        scratch_shapes=list(scratch),
        cost_estimate=pl.CostEstimate(flops=flops, bytes_accessed=moved, transcendentals=0),
        compiler_params=pltpu.CompilerParams(vmem_limit_bytes=limit * 1024 * 1024),
    )(*scalars, *operands, *after)


def stage(count, *refs):
    sems = refs[2 * count]
    copies = []
    for i in range(count):
        source = refs[i] if refs[i].shape == refs[count + i].shape else refs[i].at[0]
        copies.append(pltpu.make_async_copy(source, refs[count + i], sems.at[i]))
    for copy in copies:
        copy.start()
    for copy in copies:
        copy.wait()


def stage_late(count, own_ref, high_ref, *refs):
    outs, (base_ref, high_buf, sems) = refs[count : 2 * count], refs[2 * count :]
    copies = [pltpu.make_async_copy(high_ref, high_buf, sems.at[count])]
    copies += [pltpu.make_async_copy(refs[i], outs[i], sems.at[i]) for i in range(count)]
    for copy in copies:
        copy.start()
    copies[0].wait()
    base_ref[...] = high_buf[...] - own_ref[...]
    for copy in copies[1:]:
        copy.wait()


def place(me_ref, blocks, full_ref, rows):
    for mask, block in enumerate(blocks[::-1]):
        at = pl.multiple_of((me_ref[0] ^ mask) * rows, rows)
        if len(full_ref.shape) == 3:
            full_ref[:, pl.ds(at, rows), :] = block[...]
        else:
            full_ref[pl.ds(at, rows), :] = block[...]


def dot(left, right):
    return jnp.dot(left, right, preferred_element_type=F32)


def solve_local(size, me_ref, matrix_ref, *refs):
    blocks, (out_ref, full_ref) = refs[:size], refs[size:]
    place(me_ref, blocks, full_ref, blocks[0].shape[1])
    for s in range(matrix_ref.shape[0]):
        out_ref[s] = dot(matrix_ref[s], full_ref[s]).astype(BF16)


def reach_anc(size, me_row, matrix_ref, *refs):
    blocks, (out_ref, full_ref) = refs[:size], refs[size:]
    place(me_row, blocks, full_ref, blocks[0].shape[1])
    total = dot(matrix_ref[0], full_ref[0])
    for s in range(1, matrix_ref.shape[0]):
        total = total + dot(matrix_ref[s], full_ref[s])
    out_ref[...] = total.astype(BF16)


def reach_high(layers, block, me_layer, target_ref, full_ref, first_ref, high_ref, *refs):
    outs, (matrix_ref, total_ref, sems) = refs[:-3], refs[-3:]
    supers, rows, _ = high_ref.shape
    copies = [pltpu.make_async_copy(high_ref.at[s], matrix_ref.at[s - 1], sems.at[s - 1]) for s in range(1, supers)]
    for copy in copies:
        copy.start()
    total_ref[...] = jnp.zeros_like(total_ref)
    for s in range(supers):
        if s:
            copies[s - 1].wait()
        source = matrix_ref.at[s - 1] if s else first_ref
        group = min(rows // block, 4)

        @pl.loop(0, rows // block // group)
        def _(i):
            here = pl.ds(pl.multiple_of(i * group * block, group * block), group * block)
            product = dot(source[here, :], full_ref[s])
            for q in range(group):
                at = pl.multiple_of(target_ref[s, i * group + q] * block, block)
                total_ref[pl.ds(at, block), :] += product[q * block : (q + 1) * block, :]

    part = total_ref.shape[0] // layers
    outs = list(outs)
    for mask in [0, 1] + [m ^ 1 for m in range(2, layers)]:
        start = (me_layer[0] ^ mask) * part
        rows = outs[0].shape[0]
        for piece in range(part // rows):
            out = outs.pop(0)
            at = pl.multiple_of(start + piece * rows, rows)
            out[...] = total_ref[pl.ds(at, rows), :].astype(out.dtype)


def add(kept_ref, *refs):
    out_ref, rows = refs[-1], refs[0].shape[0]
    for i, ref in enumerate(refs[:-1]):
        at = pl.ds(i * rows, rows)
        out_ref[at, :] = (kept_ref[at, :].astype(F32) + ref[...].astype(F32)).astype(out_ref.dtype)


def reduce_anc(rhs_ref, left_ref, right_ref, out_ref):
    out_ref[...] = (rhs_ref[...] - (left_ref[...].astype(F32) + right_ref[...].astype(F32))).astype(BF16)


def solve_anc(size, me_row, matrix_ref, *refs):
    blocks, (sol_out, full_ref) = refs[:size], refs[size:]
    place(me_row, blocks, full_ref, blocks[0].shape[0])
    sol_out[...] = dot(matrix_ref[...], full_ref[...]).astype(BF16)


def sum_high(base_ref, *refs):
    parts, out_ref = refs[:-1], refs[-1]
    total = base_ref[...]
    for part in parts:
        total = total - part[...].astype(F32)
    out_ref[...] = total


def finish(size, me_row, sol_ref, base_ref, near_ref, matrix_ref, *refs):
    blocks, (sol_out, anc_out, high_out, full_ref) = refs[:size], refs[size:]
    sol_out[...] = sol_ref[...]
    anc_out[...] = blocks[-1][...]
    place(me_row, blocks, full_ref, blocks[0].shape[0])
    high_out[...] = base_ref[...] - near_ref[...].astype(F32) - dot(matrix_ref[...], full_ref[...])


def on_device(
    rows_n,
    layers_n,
    rhs_local,
    dinv_local,
    lower_anc,
    lower_high,
    row_blocks,
    rhs_anc,
    rhs_high,
    dinv_anc,
    lower_anc_high,
):
    rhs_mine, blocks_mine = rhs_local[0], row_blocks[0]
    me_row = lax.axis_index("row").astype(jnp.int32).reshape(1)
    me_layer = lax.axis_index("layer").astype(jnp.int32).reshape(1)
    shape = jax.ShapeDtypeStruct

    in_hbm = lambda x: pltpu.with_memory_space_constraint(x, pltpu.HBM)
    weights = [in_hbm(w) for w in (dinv_local[0], lower_anc[0], rhs_mine)]
    dinv_mine, anc_mine, rhs_own = call(
        functools.partial(stage, len(weights)),
        [shape(w.shape, w.dtype) for w in weights],
        weights,
        scratch=[pltpu.SemaphoreType.DMA((len(weights),))],
        specs=[HBM] * len(weights),
    )
    high_mine = lower_high[0]
    supers, order, width = rhs_mine.shape[0], dinv_mine.shape[2], rhs_mine.shape[2]
    block = high_mine.shape[1] // blocks_mine.shape[1]
    held = rhs_high.shape[0]
    full = (supers, order, width)

    rhs_blocks = gather_row(rhs_mine, rows_n, dinv_mine)
    sol_mine = call(
        functools.partial(solve_local, rows_n),
        shape(rhs_mine.shape, BF16),
        (dinv_mine, *rhs_blocks[:-1], rhs_own),
        (me_row,),
        [pltpu.VMEM(full, BF16)],
        2 * dinv_mine.size * width,
    )
    high_first, = call(
        functools.partial(stage, 1),
        [shape(high_mine.shape[1:], BF16)],
        [in_hbm(high_mine)],
        scratch=[pltpu.SemaphoreType.DMA((1,))],
        specs=[HBM],
        after=(sol_mine,),
    )
    sol_blocks = gather_row(sol_mine, rows_n, high_first)
    anc_sum, sol_full = call(
        functools.partial(reach_anc, rows_n),
        (shape((anc_mine.shape[1], width), BF16), shape(full, BF16)),
        (anc_mine, *sol_blocks),
        (me_row,),
        flops=2 * anc_mine.size * width,
    )
    kept, sent = [shape((held, width), F32)], [shape((held, width), BF16)]
    pieces = [shape((held // CHUNKS, width), BF16)] * CHUNKS
    own, near, *others = call(
        functools.partial(reach_high, layers_n, block),
        kept + sent + (kept + pieces) * (layers_n // 2 - 1),
        (sol_full, high_first, in_hbm(high_mine)),
        (me_layer, blocks_mine),
        [
            pltpu.VMEM((supers - 1, *high_mine.shape[1:]), BF16),
            pltpu.VMEM((held * layers_n, width), F32),
            pltpu.SemaphoreType.DMA((supers - 1,)),
        ],
        2 * high_mine.size * width,
        specs=[VMEM, VMEM, HBM],
    )
    mask = 1
    while mask < layers_n:
        other = swap(anc_sum, "layer", layers_n, mask)
        mask = 2 * mask + 1
        if mask < layers_n:
            anc_sum = call(add, shape(anc_sum.shape, BF16), (anc_sum, other))
    late = [in_hbm(w) for w in (rhs_anc, dinv_anc, lower_anc_high)]
    rhs_anc, dinv_anc, lower_anc_high, base = call(
        functools.partial(stage_late, len(late)),
        [shape(w.shape, w.dtype) for w in late] + [shape(rhs_high.shape, F32)],
        [own, in_hbm(rhs_high), *late],
        scratch=[pltpu.VMEM(rhs_high.shape, F32), pltpu.SemaphoreType.DMA((len(late) + 1,))],
        specs=[VMEM] + [HBM] * (1 + len(late)),
    )
    anc_rhs = call(reduce_anc, shape(rhs_anc.shape, BF16), (rhs_anc, anc_sum, other))
    received, near = [], swap(near, "layer", layers_n, 1)
    for mask in range(3, layers_n, 2):
        mine, *far = others[: 1 + CHUNKS]
        others = others[1 + CHUNKS :]
        far = [swap(piece, "layer", layers_n, 1) for piece in far]
        received.append(swap(call(add, sent[0], (mine, *far)), "layer", layers_n, mask))

    anc_solved = call(
        functools.partial(solve_anc, rows_n),
        shape(rhs_anc.shape, BF16),
        (dinv_anc, *gather_row(anc_rhs, rows_n)),
        (me_row,),
        [pltpu.VMEM((order, width), BF16)],
        2 * dinv_anc.size * width,
    )
    base = call(sum_high, shape(rhs_high.shape, F32), (base, *received))
    sol_out, anc_out, high_new = call(
        functools.partial(finish, rows_n),
        [shape(sol_mine.shape, BF16), shape(rhs_anc.shape, BF16), shape(rhs_high.shape, F32)],
        (sol_mine, base, near, lower_anc_high, *gather_row(anc_solved, rows_n)),
        (me_row,),
        [pltpu.VMEM((order, width), BF16)],
        2 * lower_anc_high.size * width,
    )
    return (sol_out[None], anc_out, high_new)


def solution(mesh):
    return jax.shard_map(
        functools.partial(on_device, mesh.shape["row"], mesh.shape["layer"]),
        mesh=mesh,
        in_specs=(
            P("layer", None, "row", None),
            P("layer", None, "row", None),
            P("layer", None, "row", None),
            P("layer", None, "row", None),
            P("layer", None, "row"),
            P("row", None),
            P(("row", "layer"), None),
            P("row", None),
            P(("row", "layer"), None),
        ),
        out_specs=(P("layer", None, "row", None), P("row", None), P(("row", "layer"), None)),
        check_vma=False,
    )
```

```python
import functools

import jax
import jax.numpy as jnp
from jax import lax
from jax.experimental import pallas as pl
from jax.experimental.pallas import tpu as pltpu
from jax.sharding import PartitionSpec as P

F32 = jnp.float32
BF16 = jnp.bfloat16
VMEM = pl.BlockSpec(memory_space=pltpu.VMEM)
SMEM = pl.BlockSpec(memory_space=pltpu.SMEM)
ANY = pl.BlockSpec(memory_space=pl.ANY)
HBM = pl.BlockSpec(memory_space=pltpu.HBM)
CHUNKS = 1


def swap(value, axis, size, mask):
    return lax.ppermute(value, axis, [(i, i ^ mask) for i in range(size)])


def gather_row(value, size, after=None):
    blocks = {0: value}
    for mask in range(2, size, 2):
        blocks[mask] = swap(value, "row", size, mask)
    blocks[1] = swap(value, "row", size, 1)
    for mask in range(2, size, 2):
        if after is not None and mask == 2:
            blocks[mask], _ = lax.optimization_barrier((blocks[mask], after))
        blocks[mask + 1] = swap(blocks[mask], "row", size, 1)
    return [blocks[mask] for mask in reversed(range(size))]


def call(body, outs, operands, scalars=(), scratch=(), flops=0, after=(), specs=None, limit=16):
    count, waits = len(scalars) + len(operands), len(after)

    def kernel(*refs):
        body(*refs[:count], *refs[count + waits :])

    moved = sum(o.size * o.dtype.itemsize for o in operands)
    return pl.pallas_call(
        kernel,
        out_shape=outs,
        in_specs=[SMEM] * len(scalars) + (specs or [VMEM] * len(operands)) + [ANY] * waits,
        out_specs=jax.tree.map(lambda _: VMEM, outs),
        scratch_shapes=list(scratch),
        cost_estimate=pl.CostEstimate(flops=flops, bytes_accessed=moved, transcendentals=0),
        compiler_params=pltpu.CompilerParams(vmem_limit_bytes=limit * 1024 * 1024),
    )(*scalars, *operands, *after)


def stage(count, *refs):
    sems = refs[2 * count]
    copies = []
    for i in range(count):
        source = refs[i] if refs[i].shape == refs[count + i].shape else refs[i].at[0]
        copies.append(pltpu.make_async_copy(source, refs[count + i], sems.at[i]))
    for copy in copies:
        copy.start()
    for copy in copies:
        copy.wait()


def stage_late(count, own_ref, high_ref, *refs):
    outs, (base_ref, high_buf, sems) = refs[count : 2 * count], refs[2 * count :]
    copies = [pltpu.make_async_copy(high_ref, high_buf, sems.at[count])]
    copies += [pltpu.make_async_copy(refs[i], outs[i], sems.at[i]) for i in range(count)]
    for copy in copies:
        copy.start()
    copies[0].wait()
    base_ref[...] = high_buf[...] - own_ref[...]
    for copy in copies[1:]:
        copy.wait()


def place(me_ref, blocks, full_ref, rows):
    for mask, block in enumerate(blocks[::-1]):
        at = pl.multiple_of((me_ref[0] ^ mask) * rows, rows)
        if len(full_ref.shape) == 3:
            full_ref[:, pl.ds(at, rows), :] = block[...]
        else:
            full_ref[pl.ds(at, rows), :] = block[...]


def dot(left, right):
    return jnp.dot(left, right, preferred_element_type=F32)


def solve_local(size, me_ref, matrix_ref, *refs):
    blocks, (out_ref, full_ref) = refs[:size], refs[size:]
    place(me_ref, blocks, full_ref, blocks[0].shape[1])
    for s in range(matrix_ref.shape[0]):
        out_ref[s] = dot(matrix_ref[s], full_ref[s]).astype(BF16)


def reach_anc(size, me_row, matrix_ref, *refs):
    blocks, (out_ref, full_ref) = refs[:size], refs[size:]
    place(me_row, blocks, full_ref, blocks[0].shape[1])
    total = dot(matrix_ref[0], full_ref[0])
    for s in range(1, matrix_ref.shape[0]):
        total = total + dot(matrix_ref[s], full_ref[s])
    out_ref[...] = total.astype(BF16)


def reach_high(layers, block, me_layer, target_ref, full_ref, first_ref, high_ref, *refs):
    outs, (matrix_ref, total_ref, sems) = refs[:-3], refs[-3:]
    supers, rows, _ = high_ref.shape
    copies = [pltpu.make_async_copy(high_ref.at[s], matrix_ref.at[s - 1], sems.at[s - 1]) for s in range(1, supers)]
    for copy in copies:
        copy.start()
    total_ref[...] = jnp.zeros_like(total_ref)
    for s in range(supers):
        if s:
            copies[s - 1].wait()
        source = matrix_ref.at[s - 1] if s else first_ref
        group = min(rows // block, 4)

        @pl.loop(0, rows // block // group)
        def _(i):
            here = pl.ds(pl.multiple_of(i * group * block, group * block), group * block)
            product = dot(source[here, :], full_ref[s])
            for q in range(group):
                at = pl.multiple_of(target_ref[s, i * group + q] * block, block)
                total_ref[pl.ds(at, block), :] += product[q * block : (q + 1) * block, :]

    part = total_ref.shape[0] // layers
    outs = list(outs)
    for mask in range(layers):
        start = (me_layer[0] ^ mask) * part
        rows = outs[0].shape[0]
        for piece in range(part // rows):
            out = outs.pop(0)
            at = pl.multiple_of(start + piece * rows, rows)
            out[...] = total_ref[pl.ds(at, rows), :].astype(out.dtype)


def add(kept_ref, *refs):
    out_ref, rows = refs[-1], refs[0].shape[0]
    for i, ref in enumerate(refs[:-1]):
        at = pl.ds(i * rows, rows)
        out_ref[at, :] = (kept_ref[at, :].astype(F32) + ref[...].astype(F32)).astype(out_ref.dtype)


def tree(values):
    while len(values) > 1:
        values = [values[i] + values[i + 1] for i in range(0, len(values), 2)]
    return values[0]


def reduce_anc(rhs_ref, *refs):
    parts, out_ref = refs[:-1], refs[-1]
    out_ref[...] = (rhs_ref[...] - tree([part[...].astype(F32) for part in parts])).astype(BF16)


def solve_anc(size, me_row, matrix_ref, *refs):
    blocks, (sol_out, full_ref) = refs[:size], refs[size:]
    place(me_row, blocks, full_ref, blocks[0].shape[0])
    sol_out[...] = dot(matrix_ref[...], full_ref[...]).astype(BF16)


def sum_high(base_ref, *refs):
    parts, out_ref = refs[:-1], refs[-1]
    total = base_ref[...]
    for part in parts:
        total = total - part[...].astype(F32)
    out_ref[...] = total


def finish(size, me_row, sol_ref, base_ref, near_ref, matrix_ref, *refs):
    blocks, (sol_out, anc_out, high_out, full_ref) = refs[:size], refs[size:]
    sol_out[...] = sol_ref[...]
    anc_out[...] = blocks[-1][...]
    place(me_row, blocks, full_ref, blocks[0].shape[0])
    high_out[...] = base_ref[...] - near_ref[...].astype(F32) - dot(matrix_ref[...], full_ref[...])


def on_device(
    rows_n,
    layers_n,
    rhs_local,
    dinv_local,
    lower_anc,
    lower_high,
    row_blocks,
    rhs_anc,
    rhs_high,
    dinv_anc,
    lower_anc_high,
):
    rhs_mine, blocks_mine = rhs_local[0], row_blocks[0]
    me_row = lax.axis_index("row").astype(jnp.int32).reshape(1)
    me_layer = lax.axis_index("layer").astype(jnp.int32).reshape(1)
    shape = jax.ShapeDtypeStruct

    in_hbm = lambda x: pltpu.with_memory_space_constraint(x, pltpu.HBM)
    weights = [in_hbm(w) for w in (dinv_local[0], lower_anc[0], rhs_mine)]
    dinv_mine, anc_mine, rhs_own = call(
        functools.partial(stage, len(weights)),
        [shape(w.shape, w.dtype) for w in weights],
        weights,
        scratch=[pltpu.SemaphoreType.DMA((len(weights),))],
        specs=[HBM] * len(weights),
    )
    high_mine = lower_high[0]
    supers, order, width = rhs_mine.shape[0], dinv_mine.shape[2], rhs_mine.shape[2]
    block = high_mine.shape[1] // blocks_mine.shape[1]
    held = rhs_high.shape[0]
    full = (supers, order, width)

    rhs_blocks = gather_row(rhs_mine, rows_n, dinv_mine)
    sol_mine = call(
        functools.partial(solve_local, rows_n),
        shape(rhs_mine.shape, BF16),
        (dinv_mine, *rhs_blocks[:-1], rhs_own),
        (me_row,),
        [pltpu.VMEM(full, BF16)],
        2 * dinv_mine.size * width,
    )
    high_first, = call(
        functools.partial(stage, 1),
        [shape(high_mine.shape[1:], BF16)],
        [in_hbm(high_mine)],
        scratch=[pltpu.SemaphoreType.DMA((1,))],
        specs=[HBM],
        after=(sol_mine,),
    )
    sol_blocks = gather_row(sol_mine, rows_n, high_first)
    anc_sum, sol_full = call(
        functools.partial(reach_anc, rows_n),
        (shape((anc_mine.shape[1], width), BF16), shape(full, BF16)),
        (anc_mine, *sol_blocks),
        (me_row,),
        flops=2 * anc_mine.size * width,
    )
    kept, sent = [shape((held, width), F32)], [shape((held, width), BF16)]
    pieces = [shape((held // CHUNKS, width), BF16)] * CHUNKS
    own, near, *others = call(
        functools.partial(reach_high, layers_n, block),
        kept + sent + (kept + pieces) * (layers_n // 2 - 1),
        (sol_full, high_first, in_hbm(high_mine)),
        (me_layer, blocks_mine),
        [
            pltpu.VMEM((supers - 1, *high_mine.shape[1:]), BF16),
            pltpu.VMEM((held * layers_n, width), F32),
            pltpu.SemaphoreType.DMA((supers - 1,)),
        ],
        2 * high_mine.size * width,
        specs=[VMEM, VMEM, HBM],
    )
    anc_parts = [anc_sum] + [swap(anc_sum, "layer", layers_n, mask) for mask in range(1, layers_n)]
    received, pairs, near = [], [], swap(near, "layer", layers_n, 1)
    for mask in range(2, layers_n, 2):
        mine, *far = others[: 1 + CHUNKS]
        others = others[1 + CHUNKS :]
        far = [swap(piece, "layer", layers_n, 1) for piece in far]
        pairs.append(call(add, sent[0], (mine, *far)))
        received.append(swap(pairs[-1], "layer", layers_n, mask))

    late = [in_hbm(w) for w in (rhs_anc, dinv_anc, lower_anc_high)]
    rhs_anc, dinv_anc, lower_anc_high, base = call(
        functools.partial(stage_late, len(late)),
        [shape(w.shape, w.dtype) for w in late] + [shape(rhs_high.shape, F32)],
        [own, in_hbm(rhs_high), *late],
        scratch=[pltpu.VMEM(rhs_high.shape, F32), pltpu.SemaphoreType.DMA((len(late) + 1,))],
        specs=[VMEM] + [HBM] * (1 + len(late)),
    )
    anc_rhs = call(reduce_anc, shape(rhs_anc.shape, BF16), (rhs_anc, *anc_parts), after=pairs)
    anc_solved = call(
        functools.partial(solve_anc, rows_n),
        shape(rhs_anc.shape, BF16),
        (dinv_anc, *gather_row(anc_rhs, rows_n)),
        (me_row,),
        [pltpu.VMEM((order, width), BF16)],
        2 * dinv_anc.size * width,
    )
    base = call(sum_high, shape(rhs_high.shape, F32), (base, *received))
    sol_out, anc_out, high_new = call(
        functools.partial(finish, rows_n),
        [shape(sol_mine.shape, BF16), shape(rhs_anc.shape, BF16), shape(rhs_high.shape, F32)],
        (sol_mine, base, near, lower_anc_high, *gather_row(anc_solved, rows_n)),
        (me_row,),
        [pltpu.VMEM((order, width), BF16)],
        2 * lower_anc_high.size * width,
    )
    return (sol_out[None], anc_out, high_new)


def solution(mesh):
    return jax.shard_map(
        functools.partial(on_device, mesh.shape["row"], mesh.shape["layer"]),
        mesh=mesh,
        in_specs=(
            P("layer", None, "row", None),
            P("layer", None, "row", None),
            P("layer", None, "row", None),
            P("layer", None, "row", None),
            P("layer", None, "row"),
            P("row", None),
            P(("row", "layer"), None),
            P("row", None),
            P(("row", "layer"), None),
        ),
        out_specs=(P("layer", None, "row", None), P("row", None), P(("row", "layer"), None)),
        check_vma=False,
    )
```

```python
import functools

import jax
import jax.numpy as jnp
from jax import lax
from jax.experimental import pallas as pl
from jax.experimental.pallas import tpu as pltpu
from jax.sharding import PartitionSpec as P

F32 = jnp.float32
BF16 = jnp.bfloat16
VMEM = pl.BlockSpec(memory_space=pltpu.VMEM)
SMEM = pl.BlockSpec(memory_space=pltpu.SMEM)
ANY = pl.BlockSpec(memory_space=pl.ANY)
HBM = pl.BlockSpec(memory_space=pltpu.HBM)
CHUNKS = 2


def swap(value, axis, size, mask):
    return lax.ppermute(value, axis, [(i, i ^ mask) for i in range(size)])


def gather_row(value, size, after=None):
    blocks = {0: value}
    for mask in range(2, size, 2):
        blocks[mask] = swap(value, "row", size, mask)
    blocks[1] = swap(value, "row", size, 1)
    for mask in range(2, size, 2):
        if after is not None and mask == 2:
            blocks[mask], _ = lax.optimization_barrier((blocks[mask], after))
        blocks[mask + 1] = swap(blocks[mask], "row", size, 1)
    return [blocks[mask] for mask in reversed(range(size))]


def call(body, outs, operands, scalars=(), scratch=(), flops=0, after=(), specs=None, limit=16):
    count, waits = len(scalars) + len(operands), len(after)

    def kernel(*refs):
        body(*refs[:count], *refs[count + waits :])

    moved = sum(o.size * o.dtype.itemsize for o in operands)
    return pl.pallas_call(
        kernel,
        out_shape=outs,
        in_specs=[SMEM] * len(scalars) + (specs or [VMEM] * len(operands)) + [ANY] * waits,
        out_specs=jax.tree.map(lambda _: VMEM, outs),
        scratch_shapes=list(scratch),
        cost_estimate=pl.CostEstimate(flops=flops, bytes_accessed=moved, transcendentals=0),
        compiler_params=pltpu.CompilerParams(vmem_limit_bytes=limit * 1024 * 1024),
    )(*scalars, *operands, *after)


def stage(count, *refs):
    sems = refs[2 * count]
    copies = []
    for i in range(count):
        source = refs[i] if refs[i].shape == refs[count + i].shape else refs[i].at[0]
        copies.append(pltpu.make_async_copy(source, refs[count + i], sems.at[i]))
    for copy in copies:
        copy.start()
    for copy in copies:
        copy.wait()


def stage_late(count, own_ref, high_ref, *refs):
    outs, (base_ref, high_buf, sems) = refs[count : 2 * count], refs[2 * count :]
    copies = [pltpu.make_async_copy(high_ref, high_buf, sems.at[count])]
    copies += [pltpu.make_async_copy(refs[i], outs[i], sems.at[i]) for i in range(count)]
    for copy in copies:
        copy.start()
    copies[0].wait()
    base_ref[...] = high_buf[...] - own_ref[...]
    for copy in copies[1:]:
        copy.wait()


def place(me_ref, blocks, full_ref, rows):
    step = min(rows, 32)
    for mask, block in enumerate(blocks[::-1]):
        start = (me_ref[0] ^ mask) * rows

        @pl.loop(0, rows // step)
        def _(i):
            here = pl.ds(pl.multiple_of(i * step, step), step)
            there = pl.ds(pl.multiple_of(start + i * step, step), step)
            if len(full_ref.shape) == 3:
                full_ref[:, there, :] = block[:, here, :]
            else:
                full_ref[there, :] = block[here, :]


def dot(left, right):
    return jnp.dot(left, right, preferred_element_type=F32)


def solve_local(size, me_ref, matrix_ref, *refs):
    blocks, (out_ref, full_ref) = refs[:size], refs[size:]
    place(me_ref, blocks, full_ref, blocks[0].shape[1])

    @pl.loop(0, matrix_ref.shape[0])
    def _(s):
        out_ref[s] = dot(matrix_ref[s], full_ref[s]).astype(BF16)


def reach_anc(size, me_row, matrix_ref, *refs):
    blocks, (out_ref, full_ref, total_ref) = refs[:size], refs[size:]
    place(me_row, blocks, full_ref, blocks[0].shape[1])
    total_ref[...] = jnp.zeros_like(total_ref)

    @pl.loop(0, matrix_ref.shape[0])
    def _(s):
        total_ref[...] += dot(matrix_ref[s], full_ref[s])

    out_ref[...] = total_ref[...].astype(BF16)


def reach_high(layers, block, me_layer, target_ref, full_ref, first_ref, high_ref, *refs):
    outs, (matrix_ref, total_ref, sems) = refs[:-3], refs[-3:]
    supers, rows, _ = high_ref.shape
    copies = [pltpu.make_async_copy(high_ref.at[s], matrix_ref.at[s - 1], sems.at[s - 1]) for s in range(1, supers)]
    for copy in copies:
        copy.start()
    total_ref[...] = jnp.zeros_like(total_ref)
    for s in range(supers):
        if s:
            copies[s - 1].wait()
        source = matrix_ref.at[s - 1] if s else first_ref
        group = min(rows // block, 4)

        @pl.loop(0, rows // block // group)
        def _(i):
            here = pl.ds(pl.multiple_of(i * group * block, group * block), group * block)
            product = dot(source[here, :], full_ref[s])
            for q in range(group):
                at = pl.multiple_of(target_ref[s, i * group + q] * block, block)
                total_ref[pl.ds(at, block), :] += product[q * block : (q + 1) * block, :]

    part = total_ref.shape[0] // layers
    outs = list(outs)
    for mask in range(layers):
        start = (me_layer[0] ^ mask) * part
        rows = outs[0].shape[0]
        for piece in range(part // rows):
            out = outs.pop(0)
            at = pl.multiple_of(start + piece * rows, rows)
            out[...] = total_ref[pl.ds(at, rows), :].astype(out.dtype)


def add(kept_ref, *refs):
    out_ref, rows = refs[-1], refs[0].shape[0]
    for i, ref in enumerate(refs[:-1]):
        at = pl.ds(i * rows, rows)
        out_ref[at, :] = (kept_ref[at, :].astype(F32) + ref[...].astype(F32)).astype(out_ref.dtype)


def reduce_anc(rhs_ref, left_ref, right_ref, out_ref):
    out_ref[...] = (rhs_ref[...] - (left_ref[...].astype(F32) + right_ref[...].astype(F32))).astype(BF16)


def solve_anc(size, me_row, matrix_ref, *refs):
    blocks, (sol_out, full_ref) = refs[:size], refs[size:]
    place(me_row, blocks, full_ref, blocks[0].shape[0])
    sol_out[...] = dot(matrix_ref[...], full_ref[...]).astype(BF16)


def sum_high(base_ref, *refs):
    parts, out_ref = refs[:-1], refs[-1]
    total = base_ref[...]
    for part in parts:
        total = total - part[...].astype(F32)
    out_ref[...] = total


def finish(size, me_row, sol_ref, base_ref, near_ref, matrix_ref, *refs):
    blocks, (sol_out, anc_out, high_out, full_ref) = refs[:size], refs[size:]
    sol_out[...] = sol_ref[...]
    anc_out[...] = blocks[-1][...]
    place(me_row, blocks, full_ref, blocks[0].shape[0])
    step = min(base_ref.shape[0], 256)

    @pl.loop(0, base_ref.shape[0] // step)
    def _(i):
        here = pl.ds(pl.multiple_of(i * step, step), step)
        high_out[here, :] = base_ref[here, :] - near_ref[here, :].astype(F32) - dot(matrix_ref[here, :], full_ref[...])


def on_device(
    rows_n,
    layers_n,
    rhs_local,
    dinv_local,
    lower_anc,
    lower_high,
    row_blocks,
    rhs_anc,
    rhs_high,
    dinv_anc,
    lower_anc_high,
):
    rhs_mine, blocks_mine = rhs_local[0], row_blocks[0]
    me_row = lax.axis_index("row").astype(jnp.int32).reshape(1)
    me_layer = lax.axis_index("layer").astype(jnp.int32).reshape(1)
    shape = jax.ShapeDtypeStruct

    in_hbm = lambda x: pltpu.with_memory_space_constraint(x, pltpu.HBM)
    weights = [in_hbm(w) for w in (dinv_local[0], lower_anc[0], rhs_mine)]
    dinv_mine, anc_mine, rhs_own = call(
        functools.partial(stage, len(weights)),
        [shape(w.shape, w.dtype) for w in weights],
        weights,
        scratch=[pltpu.SemaphoreType.DMA((len(weights),))],
        specs=[HBM] * len(weights),
    )
    high_mine = lower_high[0]
    supers, order, width = rhs_mine.shape[0], dinv_mine.shape[2], rhs_mine.shape[2]
    block = high_mine.shape[1] // blocks_mine.shape[1]
    held = rhs_high.shape[0]
    full = (supers, order, width)

    rhs_blocks = gather_row(rhs_mine, rows_n, dinv_mine)
    sol_mine = call(
        functools.partial(solve_local, rows_n),
        shape(rhs_mine.shape, BF16),
        (dinv_mine, *rhs_blocks[:-1], rhs_own),
        (me_row,),
        [pltpu.VMEM(full, BF16)],
        2 * dinv_mine.size * width,
    )
    high_first, = call(
        functools.partial(stage, 1),
        [shape(high_mine.shape[1:], BF16)],
        [in_hbm(high_mine)],
        scratch=[pltpu.SemaphoreType.DMA((1,))],
        specs=[HBM],
        after=(sol_mine,),
    )
    sol_blocks = gather_row(sol_mine, rows_n, high_first)
    anc_sum, sol_full = call(
        functools.partial(reach_anc, rows_n),
        (shape((anc_mine.shape[1], width), BF16), shape(full, BF16)),
        (anc_mine, *sol_blocks),
        (me_row,),
        [pltpu.VMEM((anc_mine.shape[1], width), F32)],
        flops=2 * anc_mine.size * width,
    )
    kept, sent = [shape((held, width), F32)], [shape((held, width), BF16)]
    pieces = [shape((held // CHUNKS, width), BF16)] * CHUNKS
    own, near, *others = call(
        functools.partial(reach_high, layers_n, block),
        kept + sent + (kept + pieces) * (layers_n // 2 - 1),
        (sol_full, high_first, in_hbm(high_mine)),
        (me_layer, blocks_mine),
        [
            pltpu.VMEM((supers - 1, *high_mine.shape[1:]), BF16),
            pltpu.VMEM((held * layers_n, width), F32),
            pltpu.SemaphoreType.DMA((supers - 1,)),
        ],
        2 * high_mine.size * width,
        specs=[VMEM, VMEM, HBM],
    )
    mask = 1
    while mask < layers_n:
        other = swap(anc_sum, "layer", layers_n, mask)
        mask *= 2
        if mask < layers_n:
            anc_sum = call(add, shape(anc_sum.shape, BF16), (anc_sum, other))
    late = [in_hbm(w) for w in (rhs_anc, dinv_anc, lower_anc_high)]
    rhs_anc, dinv_anc, lower_anc_high, base = call(
        functools.partial(stage_late, len(late)),
        [shape(w.shape, w.dtype) for w in late] + [shape(rhs_high.shape, F32)],
        [own, in_hbm(rhs_high), *late],
        scratch=[pltpu.VMEM(rhs_high.shape, F32), pltpu.SemaphoreType.DMA((len(late) + 1,))],
        specs=[VMEM] + [HBM] * (1 + len(late)),
    )
    anc_rhs = call(reduce_anc, shape(rhs_anc.shape, BF16), (rhs_anc, anc_sum, other))
    received, near = [], swap(near, "layer", layers_n, 1)
    for mask in range(2, layers_n, 2):
        mine, *far = others[: 1 + CHUNKS]
        others = others[1 + CHUNKS :]
        far = [swap(piece, "layer", layers_n, 1) for piece in far]
        received.append(swap(call(add, sent[0], (mine, *far)), "layer", layers_n, mask))

    anc_solved = call(
        functools.partial(solve_anc, rows_n),
        shape(rhs_anc.shape, BF16),
        (dinv_anc, *gather_row(anc_rhs, rows_n)),
        (me_row,),
        [pltpu.VMEM((order, width), BF16)],
        2 * dinv_anc.size * width,
    )
    base = call(sum_high, shape(rhs_high.shape, F32), (base, *received))
    sol_out, anc_out, high_new = call(
        functools.partial(finish, rows_n),
        [shape(sol_mine.shape, BF16), shape(rhs_anc.shape, BF16), shape(rhs_high.shape, F32)],
        (sol_mine, base, near, lower_anc_high, *gather_row(anc_solved, rows_n)),
        (me_row,),
        [pltpu.VMEM((order, width), BF16)],
        2 * lower_anc_high.size * width,
    )
    return (sol_out[None], anc_out, high_new)


def solution(mesh):
    return jax.shard_map(
        functools.partial(on_device, mesh.shape["row"], mesh.shape["layer"]),
        mesh=mesh,
        in_specs=(
            P("layer", None, "row", None),
            P("layer", None, "row", None),
            P("layer", None, "row", None),
            P("layer", None, "row", None),
            P("layer", None, "row"),
            P("row", None),
            P(("row", "layer"), None),
            P("row", None),
            P(("row", "layer"), None),
        ),
        out_specs=(P("layer", None, "row", None), P("row", None), P(("row", "layer"), None)),
        check_vma=False,
    )
```

```python
import functools

import jax
import jax.numpy as jnp
from jax import lax
from jax.experimental import pallas as pl
from jax.experimental.pallas import tpu as pltpu
from jax.sharding import PartitionSpec as P

F32 = jnp.float32
BF16 = jnp.bfloat16
VMEM = pl.BlockSpec(memory_space=pltpu.VMEM)
SMEM = pl.BlockSpec(memory_space=pltpu.SMEM)
ANY = pl.BlockSpec(memory_space=pl.ANY)
HBM = pl.BlockSpec(memory_space=pltpu.HBM)
CHUNKS = 2


def swap(value, axis, size, mask):
    return lax.ppermute(value, axis, [(i, i ^ mask) for i in range(size)])


def gather_row(value, size, after=None):
    blocks = {0: value}
    for mask in range(2, size, 2):
        blocks[mask] = swap(value, "row", size, mask)
    blocks[1] = swap(value, "row", size, 1)
    for mask in range(2, size, 2):
        if after is not None and mask == 2:
            blocks[mask], _ = lax.optimization_barrier((blocks[mask], after))
        blocks[mask + 1] = swap(blocks[mask], "row", size, 1)
    return [blocks[mask] for mask in reversed(range(size))]


def call(body, outs, operands, scalars=(), scratch=(), flops=0, after=(), specs=None, limit=16):
    count, waits = len(scalars) + len(operands), len(after)

    def kernel(*refs):
        body(*refs[:count], *refs[count + waits :])

    moved = sum(o.size * o.dtype.itemsize for o in operands)
    return pl.pallas_call(
        kernel,
        out_shape=outs,
        in_specs=[SMEM] * len(scalars) + (specs or [VMEM] * len(operands)) + [ANY] * waits,
        out_specs=jax.tree.map(lambda _: VMEM, outs),
        scratch_shapes=list(scratch),
        cost_estimate=pl.CostEstimate(flops=flops, bytes_accessed=moved, transcendentals=0),
        compiler_params=pltpu.CompilerParams(vmem_limit_bytes=limit * 1024 * 1024),
    )(*scalars, *operands, *after)


def stage(count, *refs):
    sems = refs[2 * count]
    copies = []
    for i in range(count):
        source = refs[i] if refs[i].shape == refs[count + i].shape else refs[i].at[0]
        copies.append(pltpu.make_async_copy(source, refs[count + i], sems.at[i]))
    for copy in copies:
        copy.start()
    for copy in copies:
        copy.wait()


def stage_late(count, own_ref, high_ref, *refs):
    outs, (base_ref, high_buf, sems) = refs[count : 2 * count], refs[2 * count :]
    copies = [pltpu.make_async_copy(high_ref, high_buf, sems.at[count])]
    copies += [pltpu.make_async_copy(refs[i], outs[i], sems.at[i]) for i in range(count)]
    for copy in copies:
        copy.start()
    copies[0].wait()
    base_ref[...] = high_buf[...] - own_ref[...]
    for copy in copies[1:]:
        copy.wait()


def place(me_ref, blocks, full_ref, rows):
    for mask, block in enumerate(blocks[::-1]):
        at = pl.multiple_of((me_ref[0] ^ mask) * rows, rows)
        if len(full_ref.shape) == 3:
            full_ref[:, pl.ds(at, rows), :] = block[...]
        else:
            full_ref[pl.ds(at, rows), :] = block[...]


def dot(left, right):
    return jnp.dot(left, right, preferred_element_type=F32)


def solve_local(size, me_ref, matrix_ref, *refs):
    blocks, (out_ref, full_ref) = refs[:size], refs[size:]
    place(me_ref, blocks, full_ref, blocks[0].shape[1])
    for s in range(matrix_ref.shape[0]):
        out_ref[s] = dot(matrix_ref[s], full_ref[s]).astype(BF16)


def reach_anc(size, me_row, matrix_ref, *refs):
    blocks, (out_ref, full_ref) = refs[:size], refs[size:]
    place(me_row, blocks, full_ref, blocks[0].shape[1])
    total = dot(matrix_ref[0], full_ref[0])
    for s in range(1, matrix_ref.shape[0]):
        total = total + dot(matrix_ref[s], full_ref[s])
    out_ref[...] = total.astype(BF16)


def reach_high(layers, block, me_layer, target_ref, full_ref, first_ref, high_ref, *refs):
    outs, (matrix_ref, total_ref, sems) = refs[:-3], refs[-3:]
    supers, rows, _ = high_ref.shape
    copies = [pltpu.make_async_copy(high_ref.at[s], matrix_ref.at[s - 1], sems.at[s - 1]) for s in range(1, supers)]
    for copy in copies:
        copy.start()
    total_ref[...] = jnp.zeros_like(total_ref)
    for s in range(supers):
        if s:
            copies[s - 1].wait()
        source = matrix_ref.at[s - 1] if s else first_ref
        group = min(rows // block, 4)

        @pl.loop(0, rows // block // group)
        def _(i):
            here = pl.ds(pl.multiple_of(i * group * block, group * block), group * block)
            product = dot(source[here, :], full_ref[s])
            for q in range(group):
                at = pl.multiple_of(target_ref[s, i * group + q] * block, block)
                total_ref[pl.ds(at, block), :] += product[q * block : (q + 1) * block, :]

    part = total_ref.shape[0] // layers
    outs = list(outs)
    for mask in range(layers):
        start = (me_layer[0] ^ mask) * part
        rows = outs[0].shape[0]
        for piece in range(part // rows):
            out = outs.pop(0)
            at = pl.multiple_of(start + piece * rows, rows)
            out[...] = total_ref[pl.ds(at, rows), :].astype(out.dtype)


def add(kept_ref, *refs):
    out_ref, rows = refs[-1], refs[0].shape[0]
    for i, ref in enumerate(refs[:-1]):
        at = pl.ds(i * rows, rows)
        out_ref[at, :] = (kept_ref[at, :].astype(F32) + ref[...].astype(F32)).astype(out_ref.dtype)


def reduce_anc(rhs_ref, left_ref, right_ref, out_ref):
    out_ref[...] = (rhs_ref[...] - (left_ref[...].astype(F32) + right_ref[...].astype(F32))).astype(BF16)


def solve_anc(size, me_row, matrix_ref, *refs):
    blocks, (sol_out, full_ref) = refs[:size], refs[size:]
    place(me_row, blocks, full_ref, blocks[0].shape[0])
    sol_out[...] = dot(matrix_ref[...], full_ref[...]).astype(BF16)


def finish(size, me_row, sol_ref, base_ref, matrix_ref, *refs):
    blocks, parts, (sol_out, anc_out, high_out, full_ref) = refs[:size], refs[size:-4], refs[-4:]
    sol_out[...] = sol_ref[...]
    anc_out[...] = blocks[-1][...]
    place(me_row, blocks, full_ref, blocks[0].shape[0])
    high = parts[0][...].astype(F32)
    for part in parts[1:]:
        high = high + part[...].astype(F32)
    high_out[...] = base_ref[...] - high - dot(matrix_ref[...], full_ref[...])


def on_device(
    rows_n,
    layers_n,
    rhs_local,
    dinv_local,
    lower_anc,
    lower_high,
    row_blocks,
    rhs_anc,
    rhs_high,
    dinv_anc,
    lower_anc_high,
):
    rhs_mine, blocks_mine = rhs_local[0], row_blocks[0]
    me_row = lax.axis_index("row").astype(jnp.int32).reshape(1)
    me_layer = lax.axis_index("layer").astype(jnp.int32).reshape(1)
    shape = jax.ShapeDtypeStruct

    in_hbm = lambda x: pltpu.with_memory_space_constraint(x, pltpu.HBM)
    weights = [in_hbm(w) for w in (dinv_local[0], lower_anc[0], rhs_mine)]
    dinv_mine, anc_mine, rhs_own = call(
        functools.partial(stage, len(weights)),
        [shape(w.shape, w.dtype) for w in weights],
        weights,
        scratch=[pltpu.SemaphoreType.DMA((len(weights),))],
        specs=[HBM] * len(weights),
    )
    high_mine = lower_high[0]
    supers, order, width = rhs_mine.shape[0], dinv_mine.shape[2], rhs_mine.shape[2]
    block = high_mine.shape[1] // blocks_mine.shape[1]
    held = rhs_high.shape[0]
    full = (supers, order, width)

    rhs_blocks = gather_row(rhs_mine, rows_n, dinv_mine)
    sol_mine = call(
        functools.partial(solve_local, rows_n),
        shape(rhs_mine.shape, BF16),
        (dinv_mine, *rhs_blocks[:-1], rhs_own),
        (me_row,),
        [pltpu.VMEM(full, BF16)],
        2 * dinv_mine.size * width,
    )
    high_first, = call(
        functools.partial(stage, 1),
        [shape(high_mine.shape[1:], BF16)],
        [in_hbm(high_mine)],
        scratch=[pltpu.SemaphoreType.DMA((1,))],
        specs=[HBM],
        after=(sol_mine,),
    )
    sol_blocks = gather_row(sol_mine, rows_n, high_first)
    anc_sum, sol_full = call(
        functools.partial(reach_anc, rows_n),
        (shape((anc_mine.shape[1], width), BF16), shape(full, BF16)),
        (anc_mine, *sol_blocks),
        (me_row,),
        flops=2 * anc_mine.size * width,
    )
    kept, sent = [shape((held, width), F32)], [shape((held, width), BF16)]
    pieces = [shape((held // CHUNKS, width), BF16)] * CHUNKS
    own, near, *others = call(
        functools.partial(reach_high, layers_n, block),
        kept + sent + (kept + pieces) * (layers_n // 2 - 1),
        (sol_full, high_first, in_hbm(high_mine)),
        (me_layer, blocks_mine),
        [
            pltpu.VMEM((supers - 1, *high_mine.shape[1:]), BF16),
            pltpu.VMEM((held * layers_n, width), F32),
            pltpu.SemaphoreType.DMA((supers - 1,)),
        ],
        2 * high_mine.size * width,
        specs=[VMEM, VMEM, HBM],
    )
    mask = 1
    while mask < layers_n:
        other = swap(anc_sum, "layer", layers_n, mask)
        mask *= 2
        if mask < layers_n:
            anc_sum = call(add, shape(anc_sum.shape, BF16), (anc_sum, other))
    late = [in_hbm(w) for w in (rhs_anc, dinv_anc, lower_anc_high)]
    rhs_anc, dinv_anc, lower_anc_high, base = call(
        functools.partial(stage_late, len(late)),
        [shape(w.shape, w.dtype) for w in late] + [shape(rhs_high.shape, F32)],
        [own, in_hbm(rhs_high), *late],
        scratch=[pltpu.VMEM(rhs_high.shape, F32), pltpu.SemaphoreType.DMA((len(late) + 1,))],
        specs=[VMEM] + [HBM] * (1 + len(late)),
    )
    anc_rhs = call(reduce_anc, shape(rhs_anc.shape, BF16), (rhs_anc, anc_sum, other))
    received, near = [], swap(near, "layer", layers_n, 1)
    for mask in range(2, layers_n, 2):
        mine, *far = others[: 1 + CHUNKS]
        others = others[1 + CHUNKS :]
        far = [swap(piece, "layer", layers_n, 1) for piece in far]
        received.append(swap(call(add, sent[0], (mine, *far)), "layer", layers_n, mask))

    anc_solved = call(
        functools.partial(solve_anc, rows_n),
        shape(rhs_anc.shape, BF16),
        (dinv_anc, *gather_row(anc_rhs, rows_n)),
        (me_row,),
        [pltpu.VMEM((order, width), BF16)],
        2 * dinv_anc.size * width,
    )
    sol_out, anc_out, high_new = call(
        functools.partial(finish, rows_n),
        [shape(sol_mine.shape, BF16), shape(rhs_anc.shape, BF16), shape(rhs_high.shape, F32)],
        (sol_mine, base, lower_anc_high, *gather_row(anc_solved, rows_n), near, *received),
        (me_row,),
        [pltpu.VMEM((order, width), BF16)],
        2 * lower_anc_high.size * width,
    )
    return (sol_out[None], anc_out, high_new)


def solution(mesh):
    return jax.shard_map(
        functools.partial(on_device, mesh.shape["row"], mesh.shape["layer"]),
        mesh=mesh,
        in_specs=(
            P("layer", None, "row", None),
            P("layer", None, "row", None),
            P("layer", None, "row", None),
            P("layer", None, "row", None),
            P("layer", None, "row"),
            P("row", None),
            P(("row", "layer"), None),
            P("row", None),
            P(("row", "layer"), None),
        ),
        out_specs=(P("layer", None, "row", None), P("row", None), P(("row", "layer"), None)),
        check_vma=False,
    )
```

```python
import functools

import jax
import jax.numpy as jnp
from jax import lax
from jax.experimental import pallas as pl
from jax.experimental.pallas import tpu as pltpu
from jax.sharding import PartitionSpec as P

F32 = jnp.float32
BF16 = jnp.bfloat16
VMEM = pl.BlockSpec(memory_space=pltpu.VMEM)
SMEM = pl.BlockSpec(memory_space=pltpu.SMEM)
ANY = pl.BlockSpec(memory_space=pl.ANY)
HBM = pl.BlockSpec(memory_space=pltpu.HBM)
CHUNKS = 1


def swap(value, axis, size, mask):
    return lax.ppermute(value, axis, [(i, i ^ mask) for i in range(size)])


def gather_row(value, size, after=None):
    blocks = {0: value}
    for mask in range(2, size, 2):
        blocks[mask] = swap(value, "row", size, mask)
    blocks[1] = swap(value, "row", size, 1)
    for mask in range(2, size, 2):
        if after is not None and mask == 2:
            blocks[mask], _ = lax.optimization_barrier((blocks[mask], after))
        blocks[mask + 1] = swap(blocks[mask], "row", size, 1)
    return [blocks[mask] for mask in reversed(range(size))]


def call(body, outs, operands, scalars=(), scratch=(), flops=0, after=(), specs=None, limit=16):
    count, waits = len(scalars) + len(operands), len(after)

    def kernel(*refs):
        body(*refs[:count], *refs[count + waits :])

    moved = sum(o.size * o.dtype.itemsize for o in operands)
    return pl.pallas_call(
        kernel,
        out_shape=outs,
        in_specs=[SMEM] * len(scalars) + (specs or [VMEM] * len(operands)) + [ANY] * waits,
        out_specs=jax.tree.map(lambda _: VMEM, outs),
        scratch_shapes=list(scratch),
        cost_estimate=pl.CostEstimate(flops=flops, bytes_accessed=moved, transcendentals=0),
        compiler_params=pltpu.CompilerParams(vmem_limit_bytes=limit * 1024 * 1024),
    )(*scalars, *operands, *after)


def stage(count, *refs):
    sems = refs[2 * count]
    copies = []
    for i in range(count):
        source = refs[i] if refs[i].shape == refs[count + i].shape else refs[i].at[0]
        copies.append(pltpu.make_async_copy(source, refs[count + i], sems.at[i]))
    for copy in copies:
        copy.start()
    for copy in copies:
        copy.wait()


def stage_late(count, own_ref, high_ref, *refs):
    outs, (base_ref, high_buf, sems) = refs[count : 2 * count], refs[2 * count :]
    copies = [pltpu.make_async_copy(high_ref, high_buf, sems.at[count])]
    copies += [pltpu.make_async_copy(refs[i], outs[i], sems.at[i]) for i in range(count)]
    for copy in copies:
        copy.start()
    copies[0].wait()
    base_ref[...] = high_buf[...] - own_ref[...]
    for copy in copies[1:]:
        copy.wait()


def place(me_ref, blocks, full_ref, rows):
    for mask, block in enumerate(blocks[::-1]):
        at = pl.multiple_of((me_ref[0] ^ mask) * rows, rows)
        if len(full_ref.shape) == 3:
            full_ref[:, pl.ds(at, rows), :] = block[...]
        else:
            full_ref[pl.ds(at, rows), :] = block[...]


def dot(left, right):
    return jnp.dot(left, right, preferred_element_type=F32)


def solve_local(size, me_ref, matrix_ref, *refs):
    blocks, (out_ref, full_ref) = refs[:size], refs[size:]
    place(me_ref, blocks, full_ref, blocks[0].shape[1])
    for s in range(matrix_ref.shape[0]):
        out_ref[s] = dot(matrix_ref[s], full_ref[s]).astype(BF16)


def reach_anc(size, me_row, matrix_ref, *refs):
    blocks, (out_ref, full_ref) = refs[:size], refs[size:]
    place(me_row, blocks, full_ref, blocks[0].shape[1])
    total = dot(matrix_ref[0], full_ref[0])
    for s in range(1, matrix_ref.shape[0]):
        total = total + dot(matrix_ref[s], full_ref[s])
    out_ref[...] = total.astype(BF16)


def reach_high(layers, block, me_layer, target_ref, full_ref, first_ref, high_ref, *refs):
    outs, (matrix_ref, total_ref, sems) = refs[:-3], refs[-3:]
    supers, rows, _ = high_ref.shape
    copies = [pltpu.make_async_copy(high_ref.at[s], matrix_ref.at[s - 1], sems.at[s - 1]) for s in range(1, supers)]
    for copy in copies:
        copy.start()
    total_ref[...] = jnp.zeros_like(total_ref)
    for s in range(supers):
        if s:
            copies[s - 1].wait()
        source = matrix_ref.at[s - 1] if s else first_ref
        group = min(rows // block, 4)

        @pl.loop(0, rows // block // group)
        def _(i):
            here = pl.ds(pl.multiple_of(i * group * block, group * block), group * block)
            product = dot(source[here, :], full_ref[s])
            for q in range(group):
                at = pl.multiple_of(target_ref[s, i * group + q] * block, block)
                total_ref[pl.ds(at, block), :] += product[q * block : (q + 1) * block, :]

    part = total_ref.shape[0] // layers
    outs = list(outs)
    for mask in range(layers):
        start = (me_layer[0] ^ mask) * part
        rows = outs[0].shape[0]
        for piece in range(part // rows):
            out = outs.pop(0)
            at = pl.multiple_of(start + piece * rows, rows)
            out[...] = total_ref[pl.ds(at, rows), :].astype(out.dtype)


def add(kept_ref, *refs):
    out_ref, rows = refs[-1], refs[0].shape[0]
    for i, ref in enumerate(refs[:-1]):
        at = pl.ds(i * rows, rows)
        out_ref[at, :] = (kept_ref[at, :].astype(F32) + ref[...].astype(F32)).astype(out_ref.dtype)


def reduce_anc(rhs_ref, left_ref, right_ref, out_ref):
    out_ref[...] = (rhs_ref[...] - (left_ref[...].astype(F32) + right_ref[...].astype(F32))).astype(BF16)


def solve_anc(size, me_row, matrix_ref, *refs):
    blocks, (sol_out, full_ref) = refs[:size], refs[size:]
    place(me_row, blocks, full_ref, blocks[0].shape[0])
    sol_out[...] = dot(matrix_ref[...], full_ref[...]).astype(BF16)


def finish(size, me_row, sol_ref, base_ref, matrix_ref, *refs):
    blocks, parts, (sol_out, anc_out, high_out, full_ref) = refs[:size], refs[size:-4], refs[-4:]
    sol_out[...] = sol_ref[...]
    anc_out[...] = blocks[-1][...]
    place(me_row, blocks, full_ref, blocks[0].shape[0])
    high = parts[0][...].astype(F32)
    for part in parts[1:]:
        high = high + part[...].astype(F32)
    high_out[...] = base_ref[...] - high - dot(matrix_ref[...], full_ref[...])


def on_device(
    rows_n,
    layers_n,
    rhs_local,
    dinv_local,
    lower_anc,
    lower_high,
    row_blocks,
    rhs_anc,
    rhs_high,
    dinv_anc,
    lower_anc_high,
):
    rhs_mine, blocks_mine = rhs_local[0], row_blocks[0]
    me_row = lax.axis_index("row").astype(jnp.int32).reshape(1)
    me_layer = lax.axis_index("layer").astype(jnp.int32).reshape(1)
    shape = jax.ShapeDtypeStruct

    in_hbm = lambda x: pltpu.with_memory_space_constraint(x, pltpu.HBM)
    weights = [in_hbm(w) for w in (dinv_local[0], lower_anc[0], rhs_mine)]
    dinv_mine, anc_mine, rhs_own = call(
        functools.partial(stage, len(weights)),
        [shape(w.shape, w.dtype) for w in weights],
        weights,
        scratch=[pltpu.SemaphoreType.DMA((len(weights),))],
        specs=[HBM] * len(weights),
    )
    high_mine = lower_high[0]
    supers, order, width = rhs_mine.shape[0], dinv_mine.shape[2], rhs_mine.shape[2]
    block = high_mine.shape[1] // blocks_mine.shape[1]
    held = rhs_high.shape[0]
    full = (supers, order, width)

    rhs_blocks = gather_row(rhs_mine, rows_n, dinv_mine)
    sol_mine = call(
        functools.partial(solve_local, rows_n),
        shape(rhs_mine.shape, BF16),
        (dinv_mine, *rhs_blocks[:-1], rhs_own),
        (me_row,),
        [pltpu.VMEM(full, BF16)],
        2 * dinv_mine.size * width,
    )
    high_first, = call(
        functools.partial(stage, 1),
        [shape(high_mine.shape[1:], BF16)],
        [in_hbm(high_mine)],
        scratch=[pltpu.SemaphoreType.DMA((1,))],
        specs=[HBM],
        after=(sol_mine,),
    )
    sol_blocks = gather_row(sol_mine, rows_n, high_first)
    anc_sum, sol_full = call(
        functools.partial(reach_anc, rows_n),
        (shape((anc_mine.shape[1], width), BF16), shape(full, BF16)),
        (anc_mine, *sol_blocks),
        (me_row,),
        flops=2 * anc_mine.size * width,
    )
    kept, sent = [shape((held, width), F32)], [shape((held, width), BF16)]
    pieces = [shape((held // CHUNKS, width), BF16)] * CHUNKS
    own, near, *others = call(
        functools.partial(reach_high, layers_n, block),
        kept + sent + (kept + pieces) * (layers_n // 2 - 1),
        (sol_full, high_first, in_hbm(high_mine)),
        (me_layer, blocks_mine),
        [
            pltpu.VMEM((supers - 1, *high_mine.shape[1:]), BF16),
            pltpu.VMEM((held * layers_n, width), F32),
            pltpu.SemaphoreType.DMA((supers - 1,)),
        ],
        2 * high_mine.size * width,
        specs=[VMEM, VMEM, HBM],
    )
    mask = 1
    while mask < layers_n:
        other = swap(anc_sum, "layer", layers_n, mask)
        mask *= 2
        if mask < layers_n:
            anc_sum = call(add, shape(anc_sum.shape, BF16), (anc_sum, other), after=(near,))
    late = [in_hbm(w) for w in (rhs_anc, dinv_anc, lower_anc_high)]
    rhs_anc, dinv_anc, lower_anc_high, base = call(
        functools.partial(stage_late, len(late)),
        [shape(w.shape, w.dtype) for w in late] + [shape(rhs_high.shape, F32)],
        [own, in_hbm(rhs_high), *late],
        scratch=[pltpu.VMEM(rhs_high.shape, F32), pltpu.SemaphoreType.DMA((len(late) + 1,))],
        specs=[VMEM] + [HBM] * (1 + len(late)),
    )
    anc_rhs = call(reduce_anc, shape(rhs_anc.shape, BF16), (rhs_anc, anc_sum, other), flops=4 * 10**9)
    received, near = [], swap(near, "layer", layers_n, 1)
    for mask in range(2, layers_n, 2):
        mine, *far = others[: 1 + CHUNKS]
        others = others[1 + CHUNKS :]
        far = [swap(piece, "layer", layers_n, 1) for piece in far]
        received.append(swap(call(add, sent[0], (mine, *far)), "layer", layers_n, mask))

    anc_solved = call(
        functools.partial(solve_anc, rows_n),
        shape(rhs_anc.shape, BF16),
        (dinv_anc, *gather_row(anc_rhs, rows_n)),
        (me_row,),
        [pltpu.VMEM((order, width), BF16)],
        2 * dinv_anc.size * width,
    )
    sol_out, anc_out, high_new = call(
        functools.partial(finish, rows_n),
        [shape(sol_mine.shape, BF16), shape(rhs_anc.shape, BF16), shape(rhs_high.shape, F32)],
        (sol_mine, base, lower_anc_high, *gather_row(anc_solved, rows_n), near, *received),
        (me_row,),
        [pltpu.VMEM((order, width), BF16)],
        2 * lower_anc_high.size * width,
    )
    return (sol_out[None], anc_out, high_new)


def solution(mesh):
    return jax.shard_map(
        functools.partial(on_device, mesh.shape["row"], mesh.shape["layer"]),
        mesh=mesh,
        in_specs=(
            P("layer", None, "row", None),
            P("layer", None, "row", None),
            P("layer", None, "row", None),
            P("layer", None, "row", None),
            P("layer", None, "row"),
            P("row", None),
            P(("row", "layer"), None),
            P("row", None),
            P(("row", "layer"), None),
        ),
        out_specs=(P("layer", None, "row", None), P("row", None), P(("row", "layer"), None)),
        check_vma=False,
    )
```

```python
import functools

import jax
import jax.numpy as jnp
from jax import lax
from jax.experimental import pallas as pl
from jax.experimental.pallas import tpu as pltpu
from jax.sharding import PartitionSpec as P

F32 = jnp.float32
BF16 = jnp.bfloat16
VMEM = pl.BlockSpec(memory_space=pltpu.VMEM)
SMEM = pl.BlockSpec(memory_space=pltpu.SMEM)
ANY = pl.BlockSpec(memory_space=pl.ANY)
HBM = pl.BlockSpec(memory_space=pltpu.HBM)
CHUNKS = 1


def swap(value, axis, size, mask):
    return lax.ppermute(value, axis, [(i, i ^ mask) for i in range(size)])


def gather_row(value, size, after=None):
    blocks = {0: value}
    for mask in range(2, size, 2):
        blocks[mask] = swap(value, "row", size, mask)
    blocks[1] = swap(value, "row", size, 1)
    for mask in range(2, size, 2):
        if after is not None and mask == 2:
            blocks[mask], _ = lax.optimization_barrier((blocks[mask], after))
        blocks[mask + 1] = swap(blocks[mask], "row", size, 1)
    return [blocks[mask] for mask in reversed(range(size))]


def call(body, outs, operands, scalars=(), scratch=(), flops=0, after=(), specs=None, limit=16):
    count, waits = len(scalars) + len(operands), len(after)

    def kernel(*refs):
        body(*refs[:count], *refs[count + waits :])

    moved = sum(o.size * o.dtype.itemsize for o in operands)
    return pl.pallas_call(
        kernel,
        out_shape=outs,
        in_specs=[SMEM] * len(scalars) + (specs or [VMEM] * len(operands)) + [ANY] * waits,
        out_specs=jax.tree.map(lambda _: VMEM, outs),
        scratch_shapes=list(scratch),
        cost_estimate=pl.CostEstimate(flops=flops, bytes_accessed=moved, transcendentals=0),
        compiler_params=pltpu.CompilerParams(vmem_limit_bytes=limit * 1024 * 1024),
    )(*scalars, *operands, *after)


def stage(count, *refs):
    sems = refs[2 * count]
    copies = []
    for i in range(count):
        source = refs[i] if refs[i].shape == refs[count + i].shape else refs[i].at[0]
        copies.append(pltpu.make_async_copy(source, refs[count + i], sems.at[i]))
    for copy in copies:
        copy.start()
    for copy in copies:
        copy.wait()


def stage_late(count, own_ref, high_ref, *refs):
    outs, (base_ref, high_buf, sems) = refs[count : 2 * count], refs[2 * count :]
    copies = [pltpu.make_async_copy(high_ref, high_buf, sems.at[count])]
    copies += [pltpu.make_async_copy(refs[i], outs[i], sems.at[i]) for i in range(count)]
    for copy in copies:
        copy.start()
    copies[0].wait()
    base_ref[...] = high_buf[...] - own_ref[...]
    for copy in copies[1:]:
        copy.wait()


def place(me_ref, blocks, full_ref, rows):
    for mask, block in enumerate(blocks[::-1]):
        at = pl.multiple_of((me_ref[0] ^ mask) * rows, rows)
        if len(full_ref.shape) == 3:
            full_ref[:, pl.ds(at, rows), :] = block[...]
        else:
            full_ref[pl.ds(at, rows), :] = block[...]


def dot(left, right):
    return jnp.dot(left, right, preferred_element_type=F32)


def solve_local(size, me_ref, matrix_ref, *refs):
    blocks, (out_ref, full_ref) = refs[:size], refs[size:]
    place(me_ref, blocks, full_ref, blocks[0].shape[1])
    for s in range(matrix_ref.shape[0]):
        out_ref[s] = dot(matrix_ref[s], full_ref[s]).astype(BF16)


def reach_anc(size, me_row, matrix_ref, *refs):
    blocks, (out_ref, full_ref) = refs[:size], refs[size:]
    place(me_row, blocks, full_ref, blocks[0].shape[1])
    total = dot(matrix_ref[0], full_ref[0])
    for s in range(1, matrix_ref.shape[0]):
        total = total + dot(matrix_ref[s], full_ref[s])
    out_ref[...] = total.astype(BF16)


def reach_high(layers, block, me_layer, target_ref, full_ref, first_ref, high_ref, *refs):
    outs, (matrix_ref, total_ref, sems) = refs[:-3], refs[-3:]
    supers, rows, _ = high_ref.shape
    copies = [pltpu.make_async_copy(high_ref.at[s], matrix_ref.at[s - 1], sems.at[s - 1]) for s in range(1, supers)]
    for copy in copies:
        copy.start()
    total_ref[...] = jnp.zeros_like(total_ref)
    for s in range(supers):
        if s:
            copies[s - 1].wait()
        source = matrix_ref.at[s - 1] if s else first_ref
        group = min(rows // block, 4)

        @pl.loop(0, rows // block // group)
        def _(i):
            here = pl.ds(pl.multiple_of(i * group * block, group * block), group * block)
            product = dot(source[here, :], full_ref[s])
            for q in range(group):
                at = pl.multiple_of(target_ref[s, i * group + q] * block, block)
                total_ref[pl.ds(at, block), :] += product[q * block : (q + 1) * block, :]

    part = total_ref.shape[0] // layers
    outs = list(outs)
    for mask in range(layers):
        start = (me_layer[0] ^ mask) * part
        rows = outs[0].shape[0]
        for piece in range(part // rows):
            out = outs.pop(0)
            at = pl.multiple_of(start + piece * rows, rows)
            out[...] = total_ref[pl.ds(at, rows), :].astype(out.dtype)


def add(kept_ref, *refs):
    out_ref, rows = refs[-1], refs[0].shape[0]
    for i, ref in enumerate(refs[:-1]):
        at = pl.ds(i * rows, rows)
        out_ref[at, :] = (kept_ref[at, :].astype(F32) + ref[...].astype(F32)).astype(out_ref.dtype)


def reduce_anc(rhs_ref, left_ref, right_ref, out_ref):
    out_ref[...] = (rhs_ref[...] - (left_ref[...].astype(F32) + right_ref[...].astype(F32))).astype(BF16)


def solve_anc(size, me_row, matrix_ref, *refs):
    blocks, (sol_out, full_ref) = refs[:size], refs[size:]
    place(me_row, blocks, full_ref, blocks[0].shape[0])
    sol_out[...] = dot(matrix_ref[...], full_ref[...]).astype(BF16)


def finish(size, me_row, sol_ref, base_ref, matrix_ref, *refs):
    blocks, parts, (sol_out, anc_out, high_out, full_ref) = refs[:size], refs[size:-4], refs[-4:]
    sol_out[...] = sol_ref[...]
    anc_out[...] = blocks[-1][...]
    place(me_row, blocks, full_ref, blocks[0].shape[0])
    high = parts[0][...].astype(F32)
    for part in parts[1:]:
        high = high + part[...].astype(F32)
    high_out[...] = base_ref[...] - high - dot(matrix_ref[...], full_ref[...])


def on_device(
    rows_n,
    layers_n,
    rhs_local,
    dinv_local,
    lower_anc,
    lower_high,
    row_blocks,
    rhs_anc,
    rhs_high,
    dinv_anc,
    lower_anc_high,
):
    rhs_mine, blocks_mine = rhs_local[0], row_blocks[0]
    me_row = lax.axis_index("row").astype(jnp.int32).reshape(1)
    me_layer = lax.axis_index("layer").astype(jnp.int32).reshape(1)
    shape = jax.ShapeDtypeStruct

    in_hbm = lambda x: pltpu.with_memory_space_constraint(x, pltpu.HBM)
    weights = [in_hbm(w) for w in (dinv_local[0], lower_anc[0], rhs_mine)]
    dinv_mine, anc_mine, rhs_own = call(
        functools.partial(stage, len(weights)),
        [shape(w.shape, w.dtype) for w in weights],
        weights,
        scratch=[pltpu.SemaphoreType.DMA((len(weights),))],
        specs=[HBM] * len(weights),
    )
    high_mine = lower_high[0]
    supers, order, width = rhs_mine.shape[0], dinv_mine.shape[2], rhs_mine.shape[2]
    block = high_mine.shape[1] // blocks_mine.shape[1]
    held = rhs_high.shape[0]
    full = (supers, order, width)

    rhs_blocks = gather_row(rhs_mine, rows_n, dinv_mine)
    sol_mine = call(
        functools.partial(solve_local, rows_n),
        shape(rhs_mine.shape, BF16),
        (dinv_mine, *rhs_blocks[:-1], rhs_own),
        (me_row,),
        [pltpu.VMEM(full, BF16)],
        2 * dinv_mine.size * width,
    )
    high_first, = call(
        functools.partial(stage, 1),
        [shape(high_mine.shape[1:], BF16)],
        [in_hbm(high_mine)],
        scratch=[pltpu.SemaphoreType.DMA((1,))],
        specs=[HBM],
        after=(sol_mine,),
    )
    sol_blocks = gather_row(sol_mine, rows_n, high_first)
    anc_sum, sol_full = call(
        functools.partial(reach_anc, rows_n),
        (shape((anc_mine.shape[1], width), BF16), shape(full, BF16)),
        (anc_mine, *sol_blocks),
        (me_row,),
        flops=2 * anc_mine.size * width,
    )
    kept, sent = [shape((held, width), F32)], [shape((held, width), BF16)]
    pieces = [shape((held // CHUNKS, width), BF16)] * CHUNKS
    own, near, *others = call(
        functools.partial(reach_high, layers_n, block),
        kept + sent + (kept + pieces) * (layers_n // 2 - 1),
        (sol_full, high_first, in_hbm(high_mine)),
        (me_layer, blocks_mine),
        [
            pltpu.VMEM((supers - 1, *high_mine.shape[1:]), BF16),
            pltpu.VMEM((held * layers_n, width), F32),
            pltpu.SemaphoreType.DMA((supers - 1,)),
        ],
        2 * high_mine.size * width,
        specs=[VMEM, VMEM, HBM],
    )
    mask = 1
    while mask < layers_n:
        other = swap(anc_sum, "layer", layers_n, mask)
        mask *= 2
        if mask < layers_n:
            anc_sum = call(add, shape(anc_sum.shape, BF16), (anc_sum, other), after=(near,))
    late = [in_hbm(w) for w in (rhs_anc, dinv_anc, lower_anc_high)]
    rhs_anc, dinv_anc, lower_anc_high, base = call(
        functools.partial(stage_late, len(late)),
        [shape(w.shape, w.dtype) for w in late] + [shape(rhs_high.shape, F32)],
        [own, in_hbm(rhs_high), *late],
        scratch=[pltpu.VMEM(rhs_high.shape, F32), pltpu.SemaphoreType.DMA((len(late) + 1,))],
        specs=[VMEM] + [HBM] * (1 + len(late)),
    )
    anc_rhs = call(reduce_anc, shape(rhs_anc.shape, BF16), (rhs_anc, anc_sum, other), flops=4 * 10**9)
    near, base = lax.optimization_barrier((near, base))
    received, near = [], swap(near, "layer", layers_n, 1)
    for mask in range(2, layers_n, 2):
        mine, *far = others[: 1 + CHUNKS]
        others = others[1 + CHUNKS :]
        far = [swap(piece, "layer", layers_n, 1) for piece in far]
        received.append(swap(call(add, sent[0], (mine, *far)), "layer", layers_n, mask))

    anc_solved = call(
        functools.partial(solve_anc, rows_n),
        shape(rhs_anc.shape, BF16),
        (dinv_anc, *gather_row(anc_rhs, rows_n)),
        (me_row,),
        [pltpu.VMEM((order, width), BF16)],
        2 * dinv_anc.size * width,
    )
    sol_out, anc_out, high_new = call(
        functools.partial(finish, rows_n),
        [shape(sol_mine.shape, BF16), shape(rhs_anc.shape, BF16), shape(rhs_high.shape, F32)],
        (sol_mine, base, lower_anc_high, *gather_row(anc_solved, rows_n), *received, near),
        (me_row,),
        [pltpu.VMEM((order, width), BF16)],
        2 * lower_anc_high.size * width,
    )
    return (sol_out[None], anc_out, high_new)


def solution(mesh):
    return jax.shard_map(
        functools.partial(on_device, mesh.shape["row"], mesh.shape["layer"]),
        mesh=mesh,
        in_specs=(
            P("layer", None, "row", None),
            P("layer", None, "row", None),
            P("layer", None, "row", None),
            P("layer", None, "row", None),
            P("layer", None, "row"),
            P("row", None),
            P(("row", "layer"), None),
            P("row", None),
            P(("row", "layer"), None),
        ),
        out_specs=(P("layer", None, "row", None), P("row", None), P(("row", "layer"), None)),
        check_vma=False,
    )
```

```python
import functools

import jax
import jax.numpy as jnp
from jax import lax
from jax.experimental import pallas as pl
from jax.experimental.pallas import tpu as pltpu
from jax.sharding import PartitionSpec as P

F32 = jnp.float32
BF16 = jnp.bfloat16
VMEM = pl.BlockSpec(memory_space=pltpu.VMEM)
SMEM = pl.BlockSpec(memory_space=pltpu.SMEM)
ANY = pl.BlockSpec(memory_space=pl.ANY)
HBM = pl.BlockSpec(memory_space=pltpu.HBM)
CHUNKS = 1


def swap(value, axis, size, mask):
    return lax.ppermute(value, axis, [(i, i ^ mask) for i in range(size)])


def gather_row(value, size, after=None, lazy=False):
    blocks = {0: value}
    for mask in range(2, size, 2):
        blocks[mask] = swap(value, "row", size, mask)
    if lazy and size > 2:
        own, blocks[2] = lax.optimization_barrier((value, blocks[2]))
        blocks[1] = swap(own, "row", size, 1)
    else:
        blocks[1] = swap(value, "row", size, 1)
    for mask in range(2, size, 2):
        if after is not None and mask == 2:
            blocks[mask], _ = lax.optimization_barrier((blocks[mask], after))
        blocks[mask + 1] = swap(blocks[mask], "row", size, 1)
    return [blocks[mask] for mask in reversed(range(size))]


def call(body, outs, operands, scalars=(), scratch=(), flops=0, after=(), specs=None, limit=16):
    count, waits = len(scalars) + len(operands), len(after)

    def kernel(*refs):
        body(*refs[:count], *refs[count + waits :])

    moved = sum(o.size * o.dtype.itemsize for o in operands)
    return pl.pallas_call(
        kernel,
        out_shape=outs,
        in_specs=[SMEM] * len(scalars) + (specs or [VMEM] * len(operands)) + [ANY] * waits,
        out_specs=jax.tree.map(lambda _: VMEM, outs),
        scratch_shapes=list(scratch),
        cost_estimate=pl.CostEstimate(flops=flops, bytes_accessed=moved, transcendentals=0),
        compiler_params=pltpu.CompilerParams(vmem_limit_bytes=limit * 1024 * 1024),
    )(*scalars, *operands, *after)


def stage(count, *refs):
    sems = refs[2 * count]
    copies = []
    for i in range(count):
        source = refs[i] if refs[i].shape == refs[count + i].shape else refs[i].at[0]
        copies.append(pltpu.make_async_copy(source, refs[count + i], sems.at[i]))
    for copy in copies:
        copy.start()
    for copy in copies:
        copy.wait()


def stage_late(count, own_ref, high_ref, *refs):
    outs, (base_ref, high_buf, sems) = refs[count : 2 * count], refs[2 * count :]
    copies = [pltpu.make_async_copy(high_ref, high_buf, sems.at[count])]
    copies += [pltpu.make_async_copy(refs[i], outs[i], sems.at[i]) for i in range(count)]
    for copy in copies:
        copy.start()
    copies[0].wait()
    base_ref[...] = high_buf[...] - own_ref[...]
    for copy in copies[1:]:
        copy.wait()


def place(me_ref, blocks, full_ref, rows):
    for mask, block in enumerate(blocks[::-1]):
        at = pl.multiple_of((me_ref[0] ^ mask) * rows, rows)
        if len(full_ref.shape) == 3:
            full_ref[:, pl.ds(at, rows), :] = block[...]
        else:
            full_ref[pl.ds(at, rows), :] = block[...]


def dot(left, right):
    return jnp.dot(left, right, preferred_element_type=F32)


def solve_local(size, me_ref, matrix_ref, *refs):
    blocks, (out_ref, full_ref) = refs[:size], refs[size:]
    place(me_ref, blocks, full_ref, blocks[0].shape[1])
    for s in range(matrix_ref.shape[0]):
        out_ref[s] = dot(matrix_ref[s], full_ref[s]).astype(BF16)


def reach_anc(size, me_row, matrix_ref, *refs):
    blocks, (out_ref, full_ref) = refs[:size], refs[size:]
    place(me_row, blocks, full_ref, blocks[0].shape[1])
    total = dot(matrix_ref[0], full_ref[0])
    for s in range(1, matrix_ref.shape[0]):
        total = total + dot(matrix_ref[s], full_ref[s])
    out_ref[...] = total.astype(BF16)


def reach_high(layers, block, me_layer, target_ref, full_ref, first_ref, high_ref, *refs):
    outs, (matrix_ref, total_ref, sems) = refs[:-3], refs[-3:]
    supers, rows, _ = high_ref.shape
    copies = [pltpu.make_async_copy(high_ref.at[s], matrix_ref.at[s - 1], sems.at[s - 1]) for s in range(1, supers)]
    for copy in copies:
        copy.start()
    total_ref[...] = jnp.zeros_like(total_ref)
    for s in range(supers):
        if s:
            copies[s - 1].wait()
        source = matrix_ref.at[s - 1] if s else first_ref
        group = min(rows // block, 4)

        @pl.loop(0, rows // block // group)
        def _(i):
            here = pl.ds(pl.multiple_of(i * group * block, group * block), group * block)
            product = dot(source[here, :], full_ref[s])
            for q in range(group):
                at = pl.multiple_of(target_ref[s, i * group + q] * block, block)
                total_ref[pl.ds(at, block), :] += product[q * block : (q + 1) * block, :]

    part = total_ref.shape[0] // layers
    outs = list(outs)
    for mask in range(layers):
        start = (me_layer[0] ^ mask) * part
        rows = outs[0].shape[0]
        for piece in range(part // rows):
            out = outs.pop(0)
            at = pl.multiple_of(start + piece * rows, rows)
            out[...] = total_ref[pl.ds(at, rows), :].astype(out.dtype)


def add(kept_ref, *refs):
    out_ref, rows = refs[-1], refs[0].shape[0]
    for i, ref in enumerate(refs[:-1]):
        at = pl.ds(i * rows, rows)
        out_ref[at, :] = (kept_ref[at, :].astype(F32) + ref[...].astype(F32)).astype(out_ref.dtype)


def reduce_anc(rhs_ref, left_ref, right_ref, out_ref):
    out_ref[...] = (rhs_ref[...] - (left_ref[...].astype(F32) + right_ref[...].astype(F32))).astype(BF16)


def solve_anc(size, me_row, matrix_ref, *refs):
    blocks, (sol_out, full_ref) = refs[:size], refs[size:]
    place(me_row, blocks, full_ref, blocks[0].shape[0])
    sol_out[...] = dot(matrix_ref[...], full_ref[...]).astype(BF16)


def finish(size, me_row, sol_ref, base_ref, matrix_ref, *refs):
    blocks, parts, (sol_out, anc_out, high_out, full_ref) = refs[:size], refs[size:-4], refs[-4:]
    sol_out[...] = sol_ref[...]
    anc_out[...] = blocks[-1][...]
    place(me_row, blocks, full_ref, blocks[0].shape[0])
    high = parts[0][...].astype(F32)
    for part in parts[1:]:
        high = high + part[...].astype(F32)
    high_out[...] = base_ref[...] - high - dot(matrix_ref[...], full_ref[...])


def on_device(
    rows_n,
    layers_n,
    rhs_local,
    dinv_local,
    lower_anc,
    lower_high,
    row_blocks,
    rhs_anc,
    rhs_high,
    dinv_anc,
    lower_anc_high,
):
    rhs_mine, blocks_mine = rhs_local[0], row_blocks[0]
    me_row = lax.axis_index("row").astype(jnp.int32).reshape(1)
    me_layer = lax.axis_index("layer").astype(jnp.int32).reshape(1)
    shape = jax.ShapeDtypeStruct

    in_hbm = lambda x: pltpu.with_memory_space_constraint(x, pltpu.HBM)
    weights = [in_hbm(w) for w in (dinv_local[0], lower_anc[0], rhs_mine)]
    dinv_mine, anc_mine, rhs_own = call(
        functools.partial(stage, len(weights)),
        [shape(w.shape, w.dtype) for w in weights],
        weights,
        scratch=[pltpu.SemaphoreType.DMA((len(weights),))],
        specs=[HBM] * len(weights),
    )
    high_mine = lower_high[0]
    supers, order, width = rhs_mine.shape[0], dinv_mine.shape[2], rhs_mine.shape[2]
    block = high_mine.shape[1] // blocks_mine.shape[1]
    held = rhs_high.shape[0]
    full = (supers, order, width)

    rhs_blocks = gather_row(rhs_mine, rows_n, dinv_mine)
    sol_mine = call(
        functools.partial(solve_local, rows_n),
        shape(rhs_mine.shape, BF16),
        (dinv_mine, *rhs_blocks[:-1], rhs_own),
        (me_row,),
        [pltpu.VMEM(full, BF16)],
        2 * dinv_mine.size * width,
    )
    high_first, = call(
        functools.partial(stage, 1),
        [shape(high_mine.shape[1:], BF16)],
        [in_hbm(high_mine)],
        scratch=[pltpu.SemaphoreType.DMA((1,))],
        specs=[HBM],
        after=(sol_mine,),
    )
    sol_blocks = gather_row(sol_mine, rows_n, high_first)
    anc_sum, sol_full = call(
        functools.partial(reach_anc, rows_n),
        (shape((anc_mine.shape[1], width), BF16), shape(full, BF16)),
        (anc_mine, *sol_blocks),
        (me_row,),
        flops=2 * anc_mine.size * width,
    )
    kept, sent = [shape((held, width), F32)], [shape((held, width), BF16)]
    pieces = [shape((held // CHUNKS, width), BF16)] * CHUNKS
    own, near, *others = call(
        functools.partial(reach_high, layers_n, block),
        kept + sent + (kept + pieces) * (layers_n // 2 - 1),
        (sol_full, high_first, in_hbm(high_mine)),
        (me_layer, blocks_mine),
        [
            pltpu.VMEM((supers - 1, *high_mine.shape[1:]), BF16),
            pltpu.VMEM((held * layers_n, width), F32),
            pltpu.SemaphoreType.DMA((supers - 1,)),
        ],
        2 * high_mine.size * width,
        specs=[VMEM, VMEM, HBM],
    )
    mask = 1
    while mask < layers_n:
        other = swap(anc_sum, "layer", layers_n, mask)
        mask *= 2
        if mask < layers_n:
            anc_sum = call(add, shape(anc_sum.shape, BF16), (anc_sum, other), after=(near,))
    late = [in_hbm(w) for w in (rhs_anc, dinv_anc, lower_anc_high)]
    rhs_anc, dinv_anc, lower_anc_high, base = call(
        functools.partial(stage_late, len(late)),
        [shape(w.shape, w.dtype) for w in late] + [shape(rhs_high.shape, F32)],
        [own, in_hbm(rhs_high), *late],
        scratch=[pltpu.VMEM(rhs_high.shape, F32), pltpu.SemaphoreType.DMA((len(late) + 1,))],
        specs=[VMEM] + [HBM] * (1 + len(late)),
    )
    anc_rhs = call(reduce_anc, shape(rhs_anc.shape, BF16), (rhs_anc, anc_sum, other), flops=4 * 10**9)
    near, base = lax.optimization_barrier((near, base))
    received, near = [], swap(near, "layer", layers_n, 1)
    for mask in range(2, layers_n, 2):
        mine, *far = others[: 1 + CHUNKS]
        others = others[1 + CHUNKS :]
        far = [swap(piece, "layer", layers_n, 1) for piece in far]
        received.append(swap(call(add, sent[0], (mine, *far)), "layer", layers_n, mask))

    anc_solved = call(
        functools.partial(solve_anc, rows_n),
        shape(rhs_anc.shape, BF16),
        (dinv_anc, *gather_row(anc_rhs, rows_n, lazy=True)),
        (me_row,),
        [pltpu.VMEM((order, width), BF16)],
        2 * dinv_anc.size * width,
    )
    sol_out, anc_out, high_new = call(
        functools.partial(finish, rows_n),
        [shape(sol_mine.shape, BF16), shape(rhs_anc.shape, BF16), shape(rhs_high.shape, F32)],
        (sol_mine, base, lower_anc_high, *gather_row(anc_solved, rows_n), *received, near),
        (me_row,),
        [pltpu.VMEM((order, width), BF16)],
        2 * lower_anc_high.size * width,
    )
    return (sol_out[None], anc_out, high_new)


def solution(mesh):
    return jax.shard_map(
        functools.partial(on_device, mesh.shape["row"], mesh.shape["layer"]),
        mesh=mesh,
        in_specs=(
            P("layer", None, "row", None),
            P("layer", None, "row", None),
            P("layer", None, "row", None),
            P("layer", None, "row", None),
            P("layer", None, "row"),
            P("row", None),
            P(("row", "layer"), None),
            P("row", None),
            P(("row", "layer"), None),
        ),
        out_specs=(P("layer", None, "row", None), P("row", None), P(("row", "layer"), None)),
        check_vma=False,
    )
```

```python
import functools

import jax
import jax.numpy as jnp
from jax import lax
from jax.experimental import pallas as pl
from jax.experimental.pallas import tpu as pltpu
from jax.sharding import PartitionSpec as P

F32 = jnp.float32
BF16 = jnp.bfloat16
VMEM = pl.BlockSpec(memory_space=pltpu.VMEM)
SMEM = pl.BlockSpec(memory_space=pltpu.SMEM)
ANY = pl.BlockSpec(memory_space=pl.ANY)
HBM = pl.BlockSpec(memory_space=pltpu.HBM)
CHUNKS = 1


def swap(value, axis, size, mask):
    return lax.ppermute(value, axis, [(i, i ^ mask) for i in range(size)])


def gather_row(value, size, after=None, lazy=False):
    blocks = {0: value}
    for mask in range(2, size, 2):
        blocks[mask] = swap(value, "row", size, mask)
    if lazy and size > 2:
        own, blocks[2] = lax.optimization_barrier((value, blocks[2]))
        blocks[1] = swap(own, "row", size, 1)
    else:
        blocks[1] = swap(value, "row", size, 1)
    for mask in range(2, size, 2):
        if after is not None and mask == 2:
            blocks[mask], _ = lax.optimization_barrier((blocks[mask], after))
        blocks[mask + 1] = swap(blocks[mask], "row", size, 1)
    return [blocks[mask] for mask in reversed(range(size))]


def call(body, outs, operands, scalars=(), scratch=(), flops=0, after=(), specs=None, limit=16):
    count, waits = len(scalars) + len(operands), len(after)

    def kernel(*refs):
        body(*refs[:count], *refs[count + waits :])

    moved = sum(o.size * o.dtype.itemsize for o in operands)
    return pl.pallas_call(
        kernel,
        out_shape=outs,
        in_specs=[SMEM] * len(scalars) + (specs or [VMEM] * len(operands)) + [ANY] * waits,
        out_specs=jax.tree.map(lambda _: VMEM, outs),
        scratch_shapes=list(scratch),
        cost_estimate=pl.CostEstimate(flops=flops, bytes_accessed=moved, transcendentals=0),
        compiler_params=pltpu.CompilerParams(vmem_limit_bytes=limit * 1024 * 1024),
    )(*scalars, *operands, *after)


def stage(count, *refs):
    sems = refs[2 * count]
    copies = []
    for i in range(count):
        source = refs[i] if refs[i].shape == refs[count + i].shape else refs[i].at[0]
        copies.append(pltpu.make_async_copy(source, refs[count + i], sems.at[i]))
    for copy in copies:
        copy.start()
    for copy in copies:
        copy.wait()


def stage_late(count, own_ref, high_ref, *refs):
    outs, (base_ref, high_buf, sems) = refs[count : 2 * count], refs[2 * count :]
    copies = [pltpu.make_async_copy(high_ref, high_buf, sems.at[count])]
    copies += [pltpu.make_async_copy(refs[i], outs[i], sems.at[i]) for i in range(count)]
    for copy in copies:
        copy.start()
    copies[0].wait()
    base_ref[...] = high_buf[...] - own_ref[...]
    for copy in copies[1:]:
        copy.wait()


def place(me_ref, blocks, full_ref, rows):
    for mask, block in enumerate(blocks[::-1]):
        at = pl.multiple_of((me_ref[0] ^ mask) * rows, rows)
        if len(full_ref.shape) == 3:
            full_ref[:, pl.ds(at, rows), :] = block[...]
        else:
            full_ref[pl.ds(at, rows), :] = block[...]


def dot(left, right):
    return jnp.dot(left, right, preferred_element_type=F32)


def solve_local(size, me_ref, matrix_ref, *refs):
    blocks, (out_ref, full_ref) = refs[:size], refs[size:]
    place(me_ref, blocks, full_ref, blocks[0].shape[1])
    for s in range(matrix_ref.shape[0]):
        out_ref[s] = dot(matrix_ref[s], full_ref[s]).astype(BF16)


def reach_anc(size, me_row, matrix_ref, *refs):
    blocks, (out_ref, full_ref) = refs[:size], refs[size:]
    place(me_row, blocks, full_ref, blocks[0].shape[1])
    total = dot(matrix_ref[0], full_ref[0])
    for s in range(1, matrix_ref.shape[0]):
        total = total + dot(matrix_ref[s], full_ref[s])
    out_ref[...] = total.astype(BF16)


def reach_high(layers, block, me_layer, target_ref, full_ref, first_ref, high_ref, *refs):
    outs, (matrix_ref, total_ref, sems) = refs[:-3], refs[-3:]
    supers, rows, _ = high_ref.shape
    copies = [pltpu.make_async_copy(high_ref.at[s], matrix_ref.at[s - 1], sems.at[s - 1]) for s in range(1, supers)]
    for copy in copies:
        copy.start()
    total_ref[...] = jnp.zeros_like(total_ref)
    for s in range(supers):
        if s:
            copies[s - 1].wait()
        source = matrix_ref.at[s - 1] if s else first_ref
        group = min(rows // block, 2)

        @pl.loop(0, rows // block // group)
        def _(i):
            here = pl.ds(pl.multiple_of(i * group * block, group * block), group * block)
            product = dot(source[here, :], full_ref[s])
            for q in range(group):
                at = pl.multiple_of(target_ref[s, i * group + q] * block, block)
                total_ref[pl.ds(at, block), :] += product[q * block : (q + 1) * block, :]

    part = total_ref.shape[0] // layers
    outs = list(outs)
    for mask in range(layers):
        start = (me_layer[0] ^ mask) * part
        rows = outs[0].shape[0]
        for piece in range(part // rows):
            out = outs.pop(0)
            at = pl.multiple_of(start + piece * rows, rows)
            out[...] = total_ref[pl.ds(at, rows), :].astype(out.dtype)


def add(kept_ref, *refs):
    out_ref, rows = refs[-1], refs[0].shape[0]
    for i, ref in enumerate(refs[:-1]):
        at = pl.ds(i * rows, rows)
        out_ref[at, :] = (kept_ref[at, :].astype(F32) + ref[...].astype(F32)).astype(out_ref.dtype)


def reduce_anc(rhs_ref, left_ref, right_ref, out_ref):
    out_ref[...] = (rhs_ref[...] - (left_ref[...].astype(F32) + right_ref[...].astype(F32))).astype(BF16)


def solve_anc(size, me_row, matrix_ref, *refs):
    blocks, (sol_out, full_ref) = refs[:size], refs[size:]
    place(me_row, blocks, full_ref, blocks[0].shape[0])
    sol_out[...] = dot(matrix_ref[...], full_ref[...]).astype(BF16)


def finish(size, me_row, sol_ref, base_ref, matrix_ref, *refs):
    blocks, parts, (sol_out, anc_out, high_out, full_ref) = refs[:size], refs[size:-4], refs[-4:]
    sol_out[...] = sol_ref[...]
    anc_out[...] = blocks[-1][...]
    place(me_row, blocks, full_ref, blocks[0].shape[0])
    high = parts[0][...].astype(F32)
    for part in parts[1:]:
        high = high + part[...].astype(F32)
    high_out[...] = base_ref[...] - high - dot(matrix_ref[...], full_ref[...])


def on_device(
    rows_n,
    layers_n,
    rhs_local,
    dinv_local,
    lower_anc,
    lower_high,
    row_blocks,
    rhs_anc,
    rhs_high,
    dinv_anc,
    lower_anc_high,
):
    rhs_mine, blocks_mine = rhs_local[0], row_blocks[0]
    me_row = lax.axis_index("row").astype(jnp.int32).reshape(1)
    me_layer = lax.axis_index("layer").astype(jnp.int32).reshape(1)
    shape = jax.ShapeDtypeStruct

    in_hbm = lambda x: pltpu.with_memory_space_constraint(x, pltpu.HBM)
    weights = [in_hbm(w) for w in (dinv_local[0], lower_anc[0], rhs_mine)]
    dinv_mine, anc_mine, rhs_own = call(
        functools.partial(stage, len(weights)),
        [shape(w.shape, w.dtype) for w in weights],
        weights,
        scratch=[pltpu.SemaphoreType.DMA((len(weights),))],
        specs=[HBM] * len(weights),
    )
    high_mine = lower_high[0]
    supers, order, width = rhs_mine.shape[0], dinv_mine.shape[2], rhs_mine.shape[2]
    block = high_mine.shape[1] // blocks_mine.shape[1]
    held = rhs_high.shape[0]
    full = (supers, order, width)

    rhs_blocks = gather_row(rhs_mine, rows_n, dinv_mine)
    sol_mine = call(
        functools.partial(solve_local, rows_n),
        shape(rhs_mine.shape, BF16),
        (dinv_mine, *rhs_blocks[:-1], rhs_own),
        (me_row,),
        [pltpu.VMEM(full, BF16)],
        2 * dinv_mine.size * width,
    )
    high_first, = call(
        functools.partial(stage, 1),
        [shape(high_mine.shape[1:], BF16)],
        [in_hbm(high_mine)],
        scratch=[pltpu.SemaphoreType.DMA((1,))],
        specs=[HBM],
        after=(sol_mine,),
    )
    sol_blocks = gather_row(sol_mine, rows_n, high_first)
    anc_sum, sol_full = call(
        functools.partial(reach_anc, rows_n),
        (shape((anc_mine.shape[1], width), BF16), shape(full, BF16)),
        (anc_mine, *sol_blocks),
        (me_row,),
        flops=2 * anc_mine.size * width,
    )
    kept, sent = [shape((held, width), F32)], [shape((held, width), BF16)]
    pieces = [shape((held // CHUNKS, width), BF16)] * CHUNKS
    own, near, *others = call(
        functools.partial(reach_high, layers_n, block),
        kept + sent + (kept + pieces) * (layers_n // 2 - 1),
        (sol_full, high_first, in_hbm(high_mine)),
        (me_layer, blocks_mine),
        [
            pltpu.VMEM((supers - 1, *high_mine.shape[1:]), BF16),
            pltpu.VMEM((held * layers_n, width), F32),
            pltpu.SemaphoreType.DMA((supers - 1,)),
        ],
        2 * high_mine.size * width,
        specs=[VMEM, VMEM, HBM],
    )
    mask = 1
    while mask < layers_n:
        other = swap(anc_sum, "layer", layers_n, mask)
        mask *= 2
        if mask < layers_n:
            anc_sum = call(add, shape(anc_sum.shape, BF16), (anc_sum, other), after=(near,))
    late = [in_hbm(w) for w in (rhs_anc, dinv_anc, lower_anc_high)]
    rhs_anc, dinv_anc, lower_anc_high, base = call(
        functools.partial(stage_late, len(late)),
        [shape(w.shape, w.dtype) for w in late] + [shape(rhs_high.shape, F32)],
        [own, in_hbm(rhs_high), *late],
        scratch=[pltpu.VMEM(rhs_high.shape, F32), pltpu.SemaphoreType.DMA((len(late) + 1,))],
        specs=[VMEM] + [HBM] * (1 + len(late)),
    )
    anc_rhs = call(reduce_anc, shape(rhs_anc.shape, BF16), (rhs_anc, anc_sum, other), flops=4 * 10**9)
    near, base = lax.optimization_barrier((near, base))
    received, near = [], swap(near, "layer", layers_n, 1)
    for mask in range(2, layers_n, 2):
        mine, *far = others[: 1 + CHUNKS]
        others = others[1 + CHUNKS :]
        far = [swap(piece, "layer", layers_n, 1) for piece in far]
        received.append(swap(call(add, sent[0], (mine, *far)), "layer", layers_n, mask))

    anc_solved = call(
        functools.partial(solve_anc, rows_n),
        shape(rhs_anc.shape, BF16),
        (dinv_anc, *gather_row(anc_rhs, rows_n, lazy=True)),
        (me_row,),
        [pltpu.VMEM((order, width), BF16)],
        2 * dinv_anc.size * width,
    )
    sol_out, anc_out, high_new = call(
        functools.partial(finish, rows_n),
        [shape(sol_mine.shape, BF16), shape(rhs_anc.shape, BF16), shape(rhs_high.shape, F32)],
        (sol_mine, base, lower_anc_high, *gather_row(anc_solved, rows_n), *received, near),
        (me_row,),
        [pltpu.VMEM((order, width), BF16)],
        2 * lower_anc_high.size * width,
    )
    return (sol_out[None], anc_out, high_new)


def solution(mesh):
    return jax.shard_map(
        functools.partial(on_device, mesh.shape["row"], mesh.shape["layer"]),
        mesh=mesh,
        in_specs=(
            P("layer", None, "row", None),
            P("layer", None, "row", None),
            P("layer", None, "row", None),
            P("layer", None, "row", None),
            P("layer", None, "row"),
            P("row", None),
            P(("row", "layer"), None),
            P("row", None),
            P(("row", "layer"), None),
        ),
        out_specs=(P("layer", None, "row", None), P("row", None), P(("row", "layer"), None)),
        check_vma=False,
    )
```

```python
import functools

import jax
import jax.numpy as jnp
from jax import lax
from jax.experimental import pallas as pl
from jax.experimental.pallas import tpu as pltpu
from jax.sharding import PartitionSpec as P

F32 = jnp.float32
BF16 = jnp.bfloat16
VMEM = pl.BlockSpec(memory_space=pltpu.VMEM)
SMEM = pl.BlockSpec(memory_space=pltpu.SMEM)
ANY = pl.BlockSpec(memory_space=pl.ANY)
HBM = pl.BlockSpec(memory_space=pltpu.HBM)
CHUNKS = 1


def swap(value, axis, size, mask):
    return lax.ppermute(value, axis, [(i, i ^ mask) for i in range(size)])


def gather_row(value, size, after=None, lazy=False):
    blocks = {0: value}
    for mask in range(2, size, 2):
        blocks[mask] = swap(value, "row", size, mask)
    if lazy and size > 2:
        own, blocks[2] = lax.optimization_barrier((value, blocks[2]))
        blocks[1] = swap(own, "row", size, 1)
    else:
        blocks[1] = swap(value, "row", size, 1)
    for mask in range(2, size, 2):
        if after is not None and mask == size - 2:
            blocks[mask], _ = lax.optimization_barrier((blocks[mask], after))
        blocks[mask + 1] = swap(blocks[mask], "row", size, 1)
    return [blocks[mask] for mask in reversed(range(size))]


def call(body, outs, operands, scalars=(), scratch=(), flops=0, after=(), specs=None, limit=16):
    count, waits = len(scalars) + len(operands), len(after)

    def kernel(*refs):
        body(*refs[:count], *refs[count + waits :])

    moved = sum(o.size * o.dtype.itemsize for o in operands)
    return pl.pallas_call(
        kernel,
        out_shape=outs,
        in_specs=[SMEM] * len(scalars) + (specs or [VMEM] * len(operands)) + [ANY] * waits,
        out_specs=jax.tree.map(lambda _: VMEM, outs),
        scratch_shapes=list(scratch),
        cost_estimate=pl.CostEstimate(flops=flops, bytes_accessed=moved, transcendentals=0),
        compiler_params=pltpu.CompilerParams(vmem_limit_bytes=limit * 1024 * 1024),
    )(*scalars, *operands, *after)


def stage(count, *refs):
    sems = refs[2 * count]
    copies = []
    for i in range(count):
        source = refs[i] if refs[i].shape == refs[count + i].shape else refs[i].at[0]
        copies.append(pltpu.make_async_copy(source, refs[count + i], sems.at[i]))
    for copy in copies:
        copy.start()
    for copy in copies:
        copy.wait()


def stage_late(count, own_ref, high_ref, *refs):
    outs, (base_ref, high_buf, sems) = refs[count : 2 * count], refs[2 * count :]
    copies = [pltpu.make_async_copy(high_ref, high_buf, sems.at[count])]
    copies += [pltpu.make_async_copy(refs[i], outs[i], sems.at[i]) for i in range(count)]
    for copy in copies:
        copy.start()
    copies[0].wait()
    base_ref[...] = high_buf[...] - own_ref[...]
    for copy in copies[1:]:
        copy.wait()


def place(me_ref, blocks, full_ref, rows):
    for mask, block in enumerate(blocks[::-1]):
        at = pl.multiple_of((me_ref[0] ^ mask) * rows, rows)
        if len(full_ref.shape) == 3:
            full_ref[:, pl.ds(at, rows), :] = block[...]
        else:
            full_ref[pl.ds(at, rows), :] = block[...]


def dot(left, right):
    return jnp.dot(left, right, preferred_element_type=F32)


def solve_local(size, me_ref, matrix_ref, *refs):
    blocks, (out_ref, full_ref) = refs[:size], refs[size:]
    place(me_ref, blocks, full_ref, blocks[0].shape[1])
    for s in range(matrix_ref.shape[0]):
        out_ref[s] = dot(matrix_ref[s], full_ref[s]).astype(BF16)


def reach_anc(size, me_row, matrix_ref, *refs):
    blocks, (out_ref, full_ref) = refs[:size], refs[size:]
    place(me_row, blocks, full_ref, blocks[0].shape[1])
    total = dot(matrix_ref[0], full_ref[0])
    for s in range(1, matrix_ref.shape[0]):
        total = total + dot(matrix_ref[s], full_ref[s])
    out_ref[...] = total.astype(BF16)


def reach_high(layers, block, me_layer, target_ref, full_ref, first_ref, high_ref, *refs):
    outs, (matrix_ref, total_ref, sems) = refs[:-3], refs[-3:]
    supers, rows, _ = high_ref.shape
    copies = [pltpu.make_async_copy(high_ref.at[s], matrix_ref.at[s - 1], sems.at[s - 1]) for s in range(1, supers)]
    for copy in copies:
        copy.start()
    total_ref[...] = jnp.zeros_like(total_ref)
    for s in range(supers):
        if s:
            copies[s - 1].wait()
        source = matrix_ref.at[s - 1] if s else first_ref
        group = min(rows // block, 4)

        @pl.loop(0, rows // block // group)
        def _(i):
            here = pl.ds(pl.multiple_of(i * group * block, group * block), group * block)
            product = dot(source[here, :], full_ref[s])
            for q in range(group):
                at = pl.multiple_of(target_ref[s, i * group + q] * block, block)
                total_ref[pl.ds(at, block), :] += product[q * block : (q + 1) * block, :]

    part = total_ref.shape[0] // layers
    outs = list(outs)
    for mask in range(layers):
        start = (me_layer[0] ^ mask) * part
        rows = outs[0].shape[0]
        for piece in range(part // rows):
            out = outs.pop(0)
            at = pl.multiple_of(start + piece * rows, rows)
            out[...] = total_ref[pl.ds(at, rows), :].astype(out.dtype)


def add(kept_ref, *refs):
    out_ref, rows = refs[-1], refs[0].shape[0]
    for i, ref in enumerate(refs[:-1]):
        at = pl.ds(i * rows, rows)
        out_ref[at, :] = (kept_ref[at, :].astype(F32) + ref[...].astype(F32)).astype(out_ref.dtype)


def reduce_anc(rhs_ref, left_ref, right_ref, out_ref):
    out_ref[...] = (rhs_ref[...] - (left_ref[...].astype(F32) + right_ref[...].astype(F32))).astype(BF16)


def solve_anc(size, me_row, matrix_ref, *refs):
    blocks, (sol_out, full_ref) = refs[:size], refs[size:]
    place(me_row, blocks, full_ref, blocks[0].shape[0])
    sol_out[...] = dot(matrix_ref[...], full_ref[...]).astype(BF16)


def finish(size, me_row, sol_ref, base_ref, matrix_ref, *refs):
    blocks, parts, (sol_out, anc_out, high_out, full_ref) = refs[:size], refs[size:-4], refs[-4:]
    sol_out[...] = sol_ref[...]
    anc_out[...] = blocks[-1][...]
    place(me_row, blocks, full_ref, blocks[0].shape[0])
    high = parts[0][...].astype(F32)
    for part in parts[1:]:
        high = high + part[...].astype(F32)
    high_out[...] = base_ref[...] - high - dot(matrix_ref[...], full_ref[...])


def on_device(
    rows_n,
    layers_n,
    rhs_local,
    dinv_local,
    lower_anc,
    lower_high,
    row_blocks,
    rhs_anc,
    rhs_high,
    dinv_anc,
    lower_anc_high,
):
    rhs_mine, blocks_mine = rhs_local[0], row_blocks[0]
    me_row = lax.axis_index("row").astype(jnp.int32).reshape(1)
    me_layer = lax.axis_index("layer").astype(jnp.int32).reshape(1)
    shape = jax.ShapeDtypeStruct

    in_hbm = lambda x: pltpu.with_memory_space_constraint(x, pltpu.HBM)
    weights = [in_hbm(w) for w in (dinv_local[0], lower_anc[0], rhs_mine)]
    dinv_mine, anc_mine, rhs_own = call(
        functools.partial(stage, len(weights)),
        [shape(w.shape, w.dtype) for w in weights],
        weights,
        scratch=[pltpu.SemaphoreType.DMA((len(weights),))],
        specs=[HBM] * len(weights),
    )
    high_mine = lower_high[0]
    supers, order, width = rhs_mine.shape[0], dinv_mine.shape[2], rhs_mine.shape[2]
    block = high_mine.shape[1] // blocks_mine.shape[1]
    held = rhs_high.shape[0]
    full = (supers, order, width)

    rhs_blocks = gather_row(rhs_mine, rows_n, dinv_mine)
    sol_mine = call(
        functools.partial(solve_local, rows_n),
        shape(rhs_mine.shape, BF16),
        (dinv_mine, *rhs_blocks[:-1], rhs_own),
        (me_row,),
        [pltpu.VMEM(full, BF16)],
        2 * dinv_mine.size * width,
    )
    high_first, = call(
        functools.partial(stage, 1),
        [shape(high_mine.shape[1:], BF16)],
        [in_hbm(high_mine)],
        scratch=[pltpu.SemaphoreType.DMA((1,))],
        specs=[HBM],
        after=(sol_mine,),
    )
    sol_blocks = gather_row(sol_mine, rows_n, high_first)
    anc_sum, sol_full = call(
        functools.partial(reach_anc, rows_n),
        (shape((anc_mine.shape[1], width), BF16), shape(full, BF16)),
        (anc_mine, *sol_blocks),
        (me_row,),
        flops=2 * anc_mine.size * width,
    )
    kept, sent = [shape((held, width), F32)], [shape((held, width), BF16)]
    pieces = [shape((held // CHUNKS, width), BF16)] * CHUNKS
    own, near, *others = call(
        functools.partial(reach_high, layers_n, block),
        kept + sent + (kept + pieces) * (layers_n // 2 - 1),
        (sol_full, high_first, in_hbm(high_mine)),
        (me_layer, blocks_mine),
        [
            pltpu.VMEM((supers - 1, *high_mine.shape[1:]), BF16),
            pltpu.VMEM((held * layers_n, width), F32),
            pltpu.SemaphoreType.DMA((supers - 1,)),
        ],
        2 * high_mine.size * width,
        specs=[VMEM, VMEM, HBM],
    )
    mask = 1
    while mask < layers_n:
        other = swap(anc_sum, "layer", layers_n, mask)
        mask *= 2
        if mask < layers_n:
            anc_sum = call(add, shape(anc_sum.shape, BF16), (anc_sum, other), after=(near,))
    late = [in_hbm(w) for w in (rhs_anc, dinv_anc, lower_anc_high)]
    rhs_anc, dinv_anc, lower_anc_high, base = call(
        functools.partial(stage_late, len(late)),
        [shape(w.shape, w.dtype) for w in late] + [shape(rhs_high.shape, F32)],
        [own, in_hbm(rhs_high), *late],
        scratch=[pltpu.VMEM(rhs_high.shape, F32), pltpu.SemaphoreType.DMA((len(late) + 1,))],
        specs=[VMEM] + [HBM] * (1 + len(late)),
    )
    anc_rhs = call(reduce_anc, shape(rhs_anc.shape, BF16), (rhs_anc, anc_sum, other), flops=4 * 10**9)
    near, base = lax.optimization_barrier((near, base))
    received, near = [], swap(near, "layer", layers_n, 1)
    for mask in range(2, layers_n, 2):
        mine, *far = others[: 1 + CHUNKS]
        others = others[1 + CHUNKS :]
        far = [swap(piece, "layer", layers_n, 1) for piece in far]
        received.append(swap(call(add, sent[0], (mine, *far)), "layer", layers_n, mask))

    anc_solved = call(
        functools.partial(solve_anc, rows_n),
        shape(rhs_anc.shape, BF16),
        (dinv_anc, *gather_row(anc_rhs, rows_n, lazy=True)),
        (me_row,),
        [pltpu.VMEM((order, width), BF16)],
        2 * dinv_anc.size * width,
    )
    sol_out, anc_out, high_new = call(
        functools.partial(finish, rows_n),
        [shape(sol_mine.shape, BF16), shape(rhs_anc.shape, BF16), shape(rhs_high.shape, F32)],
        (sol_mine, base, lower_anc_high, *gather_row(anc_solved, rows_n), *received, near),
        (me_row,),
        [pltpu.VMEM((order, width), BF16)],
        2 * lower_anc_high.size * width,
    )
    return (sol_out[None], anc_out, high_new)


def solution(mesh):
    return jax.shard_map(
        functools.partial(on_device, mesh.shape["row"], mesh.shape["layer"]),
        mesh=mesh,
        in_specs=(
            P("layer", None, "row", None),
            P("layer", None, "row", None),
            P("layer", None, "row", None),
            P("layer", None, "row", None),
            P("layer", None, "row"),
            P("row", None),
            P(("row", "layer"), None),
            P("row", None),
            P(("row", "layer"), None),
        ),
        out_specs=(P("layer", None, "row", None), P("row", None), P(("row", "layer"), None)),
        check_vma=False,
    )
```
